256 devices in a mesh: seq: 8 (over z), ch: 32 (over y, x, core).
Axes of the slice: x: 4, y: 4, z: 8, core: 2. Of those that a mesh axis runs over, the one named last changes fastest.
Arguments:
- tokens: bfloat16 [1024, 4096], P('seq', 'ch'), may hold values from -6 to 6
- input_weight: bfloat16 [3, 4096, 4096], P(None, None, 'ch'), may hold values from -0.09375 to 0.09375
- output_weight: bfloat16 [4096, 4096], P('ch'), may hold values from -0.1875 to 0.1875
- filter_first: bfloat16 [64, 1536], P('ch'), may hold values from -1.5 to 1.5, as said below
- filter_second: bfloat16 [64, 1536], P('ch'), may hold values from -1.5 to 1.5, as said below
Outputs:
- output: bfloat16 [1024, 4096], P('seq', 'ch')
- future_first: float32 [512, 4096], P('seq', 'ch')
- future_second: float32 [512, 4096], P('seq', 'ch')
The draws below stay inside these ranges and needn't reach their ends.
Inputs may be any that keep to these rules, and one draw needn't show every extreme that they name: filter_first holds each head's taps, drawn independently from tap to tap. filter_second holds each head's taps, drawn independently from tap to tap.
All inputs are finite; a program needn't handle non-finite values.
Results may differ from the reference program's by a relative error of at most 0.0076.
Values may be sent and summed in bfloat16 or wider, within the bound.
A program may use at most 64 MiB of HBM per device.

```python
import math
import jax
import jax.numpy as jnp
from jax import lax

D = 4096
HEAD = 64
HEADS = 64
TOKENS = 1024
FILT = 1536


def filter_draw(key, salt):
    key = jax.random.fold_in(key, salt)
    key_noise, key_pick, key_rate = jax.random.split(key, 3)
    positions = jnp.arange(FILT, dtype=jnp.float32)
    noise = jnp.clip(jax.random.normal(key_noise, (HEADS, FILT), jnp.float32), -4.0, 4.0)
    share = 0.5
    fast = jax.random.uniform(key_pick, (HEADS,), jnp.float32) < share
    spread = jnp.exp(jax.random.uniform(key_rate, (HEADS,), jnp.float32, math.log(0.5), math.log(2.0)))
    slow_rate = spread * (-math.log(0.4) / FILT)
    fast_rate = spread / 40.0
    rate = jnp.where(fast, fast_rate, slow_rate)
    decay = jnp.exp(-2.0 * rate)
    energy = (1.0 - decay ** FILT) / (1.0 - decay)
    taps = noise * jnp.exp(-rate[:, None] * positions[None, :]) / jnp.sqrt(energy)[:, None]
    return taps.astype(jnp.bfloat16)


def draw_filter_first(key, part):
    return filter_draw(key, 11)


def draw_filter_second(key, part):
    return filter_draw(key, 23)


def raised(array, key, source, target, shards_of, factor):
    def block_of(axis_at):
        return (jnp.arange(array.shape[axis_at]) // (array.shape[axis_at] // shards_of)).reshape((-1,) + (1,) * (array.ndim - 1 - axis_at))

    first = jax.random.permutation(key, shards_of)[block_of(target)]
    second = (block_of(target) + shards_of // 2) % shards_of
    return jnp.where((block_of(source) == first) | (block_of(source) == second), factor * array, array)


def level_of(key, shape, cuts, smallest, top_value):
    def one(dim, parts):
        heights = jax.random.uniform(jax.random.fold_in(jax.random.fold_in(key, 6), dim), (parts,), jnp.float32, smallest / len(cuts), top_value / len(cuts))
        return jnp.repeat(jnp.exp(heights), shape[dim] // parts).reshape((-1,) + (1,) * (len(shape) - dim - 1))

    factor_of = one(*cuts[0])
    for cut in cuts[1:]:
        factor_of = factor_of * one(*cut)
    return factor_of


def scatter_about(key, shape, width, most, pieces=(), kind=jnp.bfloat16):
    factor_of = level_of(key, shape, pieces, -0.22, 0.18) if pieces else 1.0
    drawn = jax.random.normal(key, shape, jnp.float32) * width * factor_of
    return jnp.minimum(jnp.maximum(drawn, -most), most).astype(kind)


def heavy_noise(rng, shape, width, reach, cuts, heavy, kind=jnp.bfloat16):
    drawn = width * jax.random.normal(rng, shape, jnp.float32)
    if cuts:
        drawn = drawn * level_of(rng, shape, cuts, -0.22, 0.18)
    return jnp.clip(raised(drawn, jax.random.fold_in(rng, 3), *heavy), -reach, reach).astype(kind)


def setup_inputs(seed: int = 0) -> dict:
    seeds = jax.random.split(jax.random.key(seed), 6)
    tokens = scatter_about(seeds[0], (TOKENS, D), 1.0, 6.0, ((0, 8), (1, 32)))
    input_weight = scatter_about(seeds[1], (3, D, D), D ** -0.5, 0.09375, ((2, 32),))
    output_weight = heavy_noise(seeds[2], (D, D), D ** -0.5, 0.1875, ((0, 32),), (0, 1, 32, 2.75))
    filter_first = draw_filter_first(jax.random.fold_in(seeds[5], 71), 0)
    filter_second = draw_filter_second(jax.random.fold_in(seeds[5], 71), 0)
    return dict(tokens=tokens, input_weight=input_weight, output_weight=output_weight, filter_first=filter_first, filter_second=filter_second)


def long_conv(signal, filters):
    length = 1 << (TOKENS + FILT).bit_length()
    grouped = signal.reshape(TOKENS, HEADS, HEAD).transpose(1, 0, 2)

    def one_head(paired):
        values, taps = paired
        spectrum = jnp.fft.rfft(values, n=length, axis=0) * jnp.fft.rfft(taps, n=length)[:, None]
        return jnp.fft.irfft(spectrum, n=length, axis=0)[:FILT]

    result = lax.map(one_head, (grouped, filters))
    return result.transpose(1, 0, 2).reshape(FILT, D)


def reference(tokens, input_weight, output_weight, filter_first, filter_second):
    wide_tokens = tokens.astype(jnp.float32)
    projected = [jnp.dot(wide_tokens, input_weight[index].astype(jnp.float32)).astype(jnp.bfloat16) for index in range(3)]
    gate_one, gate_two, value = projected
    first = long_conv(value.astype(jnp.float32), filter_first.astype(jnp.float32))
    mixed_one = (gate_one.astype(jnp.float32) * first[:TOKENS]).astype(jnp.bfloat16)
    second = long_conv(mixed_one.astype(jnp.float32), filter_second.astype(jnp.float32))
    mixed_two = (gate_two.astype(jnp.float32) * second[:TOKENS]).astype(jnp.bfloat16)
    output = jnp.dot(mixed_two.astype(jnp.float32), output_weight.astype(jnp.float32)).astype(jnp.bfloat16)
    return output, first[TOKENS:].astype(jnp.float32), second[TOKENS:].astype(jnp.float32)
```

```python
import functools

import jax
import jax.numpy as jnp
from jax import lax
from jax.experimental import pallas as pl
from jax.experimental.pallas import tpu as pltpu
from jax.sharding import PartitionSpec as P

MESH = pl.DeviceIdType.MESH
B = 128
H = 64
F32 = jnp.float32
BF16 = jnp.bfloat16


def build_toeplitz(taps, matrix):
    width = taps.shape[1] + B
    padded = jnp.concatenate([jnp.zeros((1, B), F32), taps], axis=1)
    rows = jnp.broadcast_to(padded, (8, width))
    row = lax.broadcasted_iota(jnp.int32, (8, width), 0)
    for bit in (1, 2, 4):
        rows = jnp.where((row & bit) != 0, pltpu.roll(rows, bit, 1), rows)
    for pair in range(B // 16):
        low = rows if pair == 0 else pltpu.roll(rows, 16 * pair, 1)
        high = pltpu.roll(rows, 16 * pair + 8, 1)
        both = jnp.concatenate([low[:, B:], high[:, B:]], axis=0)
        matrix[16 * pair : 16 * pair + 16, :] = both.astype(BF16)


def kernel(
    q, nz, copies,
    tok, wi, wo, f1, f2,
    out, ff, fs,
    X, Wv, Wc, acc, F1v, F2v, M1, M2, S1, G, P1, P2, U2, S2, V,
    FS1, FS2, FL1, FL2, PS, OA, OB, RA, RB, QA, QB, RA2, RB2,
    ssem, rsem, lsem,
):
    cz = B // nz
    prompt = nz
    blocks = M1.shape[1] // B
    z = lax.axis_index("seq")
    ch = lax.axis_index("ch")
    core = ch % 2
    x = (ch // 2) % q
    y = ch // (2 * q)

    def ch_of(yy, xx, cc):
        return (yy * q + xx) * 2 + cc

    def xpeer(e):
        return (z, ch_of(y, (x + e) % q, core))

    def ypeer(e):
        return (z, ch_of((y + e) % q, x, core))

    sibling = (z, ch_of(y, x, 1 - core))

    def zpeer(e, cc):
        return ((z + e) % nz, ch_of(y, x, cc))

    counter = [0]
    sent = []

    def send(src, dst, device):
        i = counter[0]
        counter[0] += 1
        copy = pltpu.make_async_remote_copy(
            src_ref=src, dst_ref=dst, send_sem=ssem.at[i], recv_sem=rsem.at[i],
            device_id=device, device_id_type=MESH,
        )
        copy.start()
        sent.append(copy)
        return copy

    local_count = [0]

    def local(src, dst):
        i = local_count[0]
        local_count[0] += 1
        copy = pltpu.make_async_copy(src, dst, lsem.at[i])
        copy.start()
        return copy

    barrier = pltpu.get_barrier_semaphore()
    partners = [sibling]
    for e in range(1, q):
        partners += [xpeer(e), ypeer(e)]
    for e in range(1, nz):
        partners += [zpeer(e, core), zpeer(e, 1 - core)]
    for device in partners:
        pl.semaphore_signal(barrier, inc=1, device_id=device, device_id_type=MESH)

    own = local(tok, X.at[0, 0, 0])
    taps = [local(f1, F1v), local(f2, F2v)]
    weights = []
    for k in (2, 0, 1):
        for r in range(2):
            weights.append(
                local(
                    wi.at[k, :, core if r == 0 else 1 - core],
                    Wv.at[:, r, :, ((k + 1) % 3) * B : ((k + 1) % 3) * B + B],
                )
            )
    outw = []
    for c in range(q * q):
        outw.append(
            local(wo.at[:, pl.ds(pl.multiple_of((2 * c + core) * B, B), B)], Wc.at[c, 0])
        )
    pl.semaphore_wait(barrier, len(partners))

    ag_x = [send(tok, X.at[0, q - e, 0], xpeer(e)) for e in range(1, q)]
    ag_y = [send(tok, X.at[q - e, 0, 0], ypeer(e)) for e in range(1, q)]
    ag_s = [send(tok, X.at[0, 0, 1], sibling)]
    wo_s = []

    own.wait()
    for copy in taps:
        copy.wait()
    first_head = z * cz < H

    def head_taps(ref):
        both = ref[...].astype(F32)
        return jnp.where(first_head, both[0:1], both[1:2])

    build_toeplitz(head_taps(F1v), M1)

    for copy in ag_x:
        copy.wait_recv()
    ag_a = [
        send(X.at[0, 1:q, 0, 0:H], X.at[q - e, 1:q, 0, 0:H], ypeer(e)) for e in range(1, q)
    ]
    for copy in ag_y:
        copy.wait_recv()
    ag_b = [
        send(X.at[1:q, 0, 0, H:B], X.at[1:q, q - e, 0, H:B], xpeer(e)) for e in range(1, q)
    ]
    ag_s.append(send(X.at[0, 1:q, 0], X.at[0, 1:q, 1], sibling))
    ag_s.append(send(X.at[1:q, 0, 0], X.at[1:q, 0, 1], sibling))

    for c in range(q * q):
        wo_s.append(
            send(
                wo.at[:, pl.ds(pl.multiple_of((2 * c + 1 - core) * B, B), B)],
                Wc.at[c, 1],
                sibling,
            )
        )

    build_toeplitz(head_taps(F2v), M2)
    for copy in weights:
        copy.wait()

    def chip_of(dy, dx):
        return ((y + dy) % q) * q + (x + dx) % q

    def terms(dy, dx, cols):
        tile = jnp.concatenate([X[dy, dx, 0], X[dy, dx, 1]], axis=1)
        c = chip_of(dy, dx)
        weight = jnp.concatenate([Wv[c, 0, :, cols], Wv[c, 1, :, cols]], axis=0)
        return jnp.dot(tile, weight, preferred_element_type=F32)

    every = slice(0, 3 * B)
    for copy in ag_s:
        copy.wait_recv()
    total = terms(0, 0, every)
    for d in range(1, q):
        total += terms(0, d, every)
        total += terms(d, 0, every)
    acc[...] = total

    for e in range(1, q):
        ag_a[e - 1].wait_recv()
        ag_s.append(send(X.at[q - e, 1:q, 0, 0:H], X.at[q - e, 1:q, 1, 0:H], sibling))
        ag_b[e - 1].wait_recv()
        ag_s.append(send(X.at[1:q, q - e, 0, H:B], X.at[1:q, q - e, 1, H:B], sibling))
    for copy in ag_s[3:]:
        copy.wait_recv()

    a2a = []
    for part in range(3):
        cols = slice(part * B, part * B + B)
        total = acc[:, cols]
        for dy in range(1, q):
            for dx in range(1, q):
                total += terms(dy, dx, cols)
        flipped = jnp.transpose(total).astype(BF16)
        S1[part] = flipped.reshape(nz, cz, B)
        for e in range(1, nz):
            a2a.append(
                send(S1.at[part, (z + e) % nz], G.at[part, z], zpeer(e, core))
            )
        G[part, z] = S1[part, z]

    def received(part):
        for copy in a2a[part * (nz - 1) : (part + 1) * (nz - 1)]:
            copy.wait_recv()

    def conv_block(P_ref, t):
        total = None
        for s in range(nz):
            if 0 <= t - s < blocks:
                term = P_ref[s * cz : s * cz + cz, (t - s) * B : (t - s) * B + B]
                total = term if total is None else total + term
        return total

    received(0)
    signal = G[0].reshape(B, B)
    P1[:, : prompt * B] = jnp.dot(signal, M1[:, : prompt * B], preferred_element_type=F32)
    received(1)
    for t in range(prompt):
        mixed = (G[1, t].astype(F32) * conv_block(P1, t)).astype(BF16)
        U2[t * cz : t * cz + cz, :] = mixed
    P2[:, : prompt * B] = jnp.dot(U2[...], M2[:, : prompt * B], preferred_element_type=F32)
    received(2)
    for t in range(prompt):
        S2[t] = (G[2, t].astype(F32) * conv_block(P2, t)).astype(BF16)
    back = []
    for e in range(1, nz):
        back.append(send(S2.at[(z + e) % nz], V.at[0, z], zpeer(e, core)))
        back.append(send(S2.at[(z + e) % nz], V.at[1, z], zpeer(e, 1 - core)))
    back.append(send(S2.at[z], V.at[1, z], sibling))
    V[0, z] = S2[z]

    future = []
    for P_ref, M_ref, sig, FS, FL in ((P1, M1, signal, FS1, FL1), (P2, M2, U2[...], FS2, FL2)):
        P_ref[:, prompt * B :] = jnp.dot(sig, M_ref[:, prompt * B :], preferred_element_type=F32)
        for t in range(prompt, blocks):
            FS[t - prompt] = conv_block(P_ref, t)
        group = []
        for e in range(1, nz):
            group.append(send(FS.at[((z + e) % nz) // 2], FL.at[z], zpeer(e, core)))
        FL[z] = FS[z // 2]
        future.append(group)

    for copy in outw:
        copy.wait()
    for copy in wo_s:
        copy.wait_recv()
    for copy in back:
        copy.wait_recv()
    mixed = jnp.transpose(V[...].reshape(2 * B, B).astype(F32)).astype(BF16)
    for dx in list(range(1, q)) + [0]:
        for dy in range(q):
            c = chip_of(dy, dx)
            weight = jnp.concatenate([Wc[c, 0], Wc[c, 1]], axis=0)
            block = jnp.dot(mixed, weight, preferred_element_type=F32)
            PS[dy, dx] = block.astype(BF16)
            if dx == 0:
                OA[dy] = block[0:H]
            if dy == 0:
                OB[dx] = block[H:B]
    rs_a = [send(PS.at[:, e, 0:H], RA.at[q - e], xpeer(e)) for e in range(1, q)]
    rs_b = [send(PS.at[e, :, H:B], RB.at[q - e], ypeer(e)) for e in range(1, q)]

    def future_rows(group, FL, ref):
        for copy in group:
            copy.wait_recv()
        rows = jnp.transpose(FL[...].reshape(B, B))
        ref[...] = jnp.where(z % 2 == 0, rows[0:H], rows[H:B])

    future_rows(future[0], FL1, ff)
    future_rows(future[1], FL2, fs)

    for copy in rs_a:
        copy.wait_recv()
    for d in range(q):
        total = OA[d]
        for e in range(1, q):
            total += RA[e, d].astype(F32)
        OA[d] = total
        QA[d] = total.astype(BF16)
    rs_a2 = [send(QA.at[e], RA2.at[q - e], ypeer(e)) for e in range(1, q)]
    for copy in rs_b:
        copy.wait_recv()
    for d in range(q):
        total = OB[d]
        for e in range(1, q):
            total += RB[e, d].astype(F32)
        OB[d] = total
        QB[d] = total.astype(BF16)
    rs_b2 = [send(QB.at[e], RB2.at[q - e], xpeer(e)) for e in range(1, q)]

    for group, O, R, rows in ((rs_a2, OA, RA2, slice(0, H)), (rs_b2, OB, RB2, slice(H, B))):
        for copy in group:
            copy.wait_recv()
        total = O[0]
        for e in range(1, q):
            total += R[e].astype(F32)
        out[rows, :] = total.astype(BF16)

    for copy in sent:
        copy.wait_send()
    assert counter[0] == copies, counter[0]


def per_device(nz, tokens, input_weight, output_weight, filter_first, filter_second):
    depth, width = input_weight.shape[1:]
    chips = depth // (2 * B)
    q = int(round(chips**0.5))
    cz = B // nz
    taps = filter_first.shape[1]
    future = (taps // B - nz)
    copies = 4 * (q - 1) + 3 + q * q + 2 * (q - 1) + 3 * (nz - 1)
    copies += 2 * (nz - 1) + 1 + 2 * (nz - 1) + 4 * (q - 1)
    weights = input_weight.reshape(3, chips, 2, B, width)
    hbm = pl.BlockSpec(memory_space=pl.ANY)
    vmem = pl.BlockSpec(memory_space=pltpu.VMEM)
    scratch = [
        pltpu.VMEM((q, q, 2, B, B), BF16),
        pltpu.VMEM((chips, 2, B, 3 * B), BF16),
        pltpu.VMEM((chips, 2, B, B), BF16),
        pltpu.VMEM((B, 3 * B), F32),
        pltpu.VMEM((2, taps), BF16),
        pltpu.VMEM((2, taps), BF16),
        pltpu.VMEM((B, taps), BF16),
        pltpu.VMEM((B, taps), BF16),
        pltpu.VMEM((3, nz, cz, B), BF16),
        pltpu.VMEM((3, nz, cz, B), BF16),
        pltpu.VMEM((B, taps), F32),
        pltpu.VMEM((B, taps), F32),
        pltpu.VMEM((B, B), BF16),
        pltpu.VMEM((nz, cz, B), BF16),
        pltpu.VMEM((2, nz, cz, B), BF16),
        pltpu.VMEM((future, cz, B), F32),
        pltpu.VMEM((future, cz, B), F32),
        pltpu.VMEM((nz, cz, B), F32),
        pltpu.VMEM((nz, cz, B), F32),
        pltpu.VMEM((q, q, B, B), BF16),
        pltpu.VMEM((q, H, B), F32),
        pltpu.VMEM((q, H, B), F32),
        pltpu.VMEM((q, q, H, B), BF16),
        pltpu.VMEM((q, q, H, B), BF16),
        pltpu.VMEM((q, H, B), BF16),
        pltpu.VMEM((q, H, B), BF16),
        pltpu.VMEM((q, H, B), BF16),
        pltpu.VMEM((q, H, B), BF16),
        pltpu.SemaphoreType.DMA((copies,)),
        pltpu.SemaphoreType.DMA((copies,)),
        pltpu.SemaphoreType.DMA((9 + chips,)),
    ]
    return pl.pallas_call(
        functools.partial(kernel, q, nz, copies),
        out_shape=(
            jax.ShapeDtypeStruct((B, B), BF16),
            jax.ShapeDtypeStruct((H, B), F32),
            jax.ShapeDtypeStruct((H, B), F32),
        ),
        in_specs=[hbm] * 5,
        out_specs=(vmem, vmem, vmem),
        scratch_shapes=scratch,
        compiler_params=pltpu.CompilerParams(
            collective_id=0, has_side_effects=True, vmem_limit_bytes=32 * 2**20
        ),
    )(tokens, weights, output_weight, filter_first, filter_second)


def solution(mesh):
    in_specs = (P("seq", "ch"), P(None, None, "ch"), P("ch", None), P("ch", None), P("ch", None))
    out_specs = (P("seq", "ch"), P("seq", "ch"), P("seq", "ch"))
    return jax.shard_map(
        functools.partial(per_device, mesh.shape["seq"]),
        mesh=mesh, in_specs=in_specs, out_specs=out_specs, check_vma=False,
    )
```

```python
import functools

import jax
import jax.numpy as jnp
from jax import lax
from jax.experimental import pallas as pl
from jax.experimental.pallas import tpu as pltpu
from jax.sharding import PartitionSpec as P

MESH = pl.DeviceIdType.MESH
B = 128
H = 64
F32 = jnp.float32
BF16 = jnp.bfloat16


def build_toeplitz(taps, matrix):
    width = taps.shape[1] + B
    padded = jnp.concatenate([jnp.zeros((1, B), F32), taps], axis=1)
    rows = jnp.broadcast_to(padded, (8, width))
    row = lax.broadcasted_iota(jnp.int32, (8, width), 0)
    for bit in (1, 2, 4):
        rows = jnp.where((row & bit) != 0, pltpu.roll(rows, bit, 1), rows)
    for pair in range(B // 16):
        low = rows if pair == 0 else pltpu.roll(rows, 16 * pair, 1)
        high = pltpu.roll(rows, 16 * pair + 8, 1)
        both = jnp.concatenate([low[:, B:], high[:, B:]], axis=0)
        matrix[16 * pair : 16 * pair + 16, :] = both.astype(BF16)


def kernel(
    q, nz, copies,
    tok, wi, wo, f1, f2,
    out, ff, fs,
    X, Wv, Wc, acc, F1v, F2v, M1, M2, S0, S1, G0, G1, P1, P2, U2, S2, V,
    FS1, FS2, FL1, FL2, PS, OA, OB, RA, RB, QA, QB, RA2, RB2,
    ssem, rsem, lsem,
):
    cz = B // nz
    prompt = nz
    blocks = M1.shape[1] // B
    z = lax.axis_index("seq")
    ch = lax.axis_index("ch")
    core = ch % 2
    x = (ch // 2) % q
    y = ch // (2 * q)

    near = [1, q - 1] if q > 2 else [1]
    offsets = [0] + near + [e for e in range(2, q - 1)]
    slot_of = {e: i for i, e in enumerate(offsets)}
    groups = [(1, 1 + len(near))] + [(i, i + 1) for i in range(1 + len(near), q)]
    steps = offsets[1:]

    def land(e):
        return slot_of[q - e]

    def ch_of(yy, xx, cc):
        return (yy * q + xx) * 2 + cc

    def xpeer(e):
        return (z, ch_of(y, (x + e) % q, core))

    def ypeer(e):
        return (z, ch_of((y + e) % q, x, core))

    sibling = (z, ch_of(y, x, 1 - core))

    def zpeer(e):
        return ((z + e) % nz, ch)

    far_first = sorted(range(1, nz), key=lambda e: -min(e, nz - e))
    near_first = sorted(range(1, nz), key=lambda e: min(e, nz - e))

    counter = [0]
    sent = []

    def send(src, dst, device):
        i = counter[0]
        counter[0] += 1
        copy = pltpu.make_async_remote_copy(
            src_ref=src, dst_ref=dst, send_sem=ssem.at[i], recv_sem=rsem.at[i],
            device_id=device, device_id_type=MESH,
        )
        copy.start()
        sent.append(copy)
        return copy

    local_count = [0]

    def local(src, dst):
        i = local_count[0]
        local_count[0] += 1
        copy = pltpu.make_async_copy(src, dst, lsem.at[i])
        copy.start()
        return copy

    barrier = pltpu.get_barrier_semaphore()
    partners = [zpeer(e) for e in far_first]
    for e in range(1, q):
        partners += [xpeer(e), ypeer(e)]
    partners.append(sibling)
    for device in partners:
        pl.semaphore_signal(barrier, inc=1, device_id=device, device_id_type=MESH)

    own = local(tok, X.at[0, 0, 0])
    taps = [local(f1, F1v), local(f2, F2v)]
    weights = []
    for k, column in ((2, 0), (0, 1), (1, 2)):
        for r in range(2):
            weights.append(
                local(
                    wi.at[k, :, core if r == 0 else 1 - core],
                    Wv.at[:, r, :, column * B : column * B + B],
                )
            )
    pl.semaphore_wait(barrier, len(partners))

    ag_x, ag_y = {}, {}
    for e in steps:
        ag_x[e] = send(tok, X.at[0, land(e), 0], xpeer(e))
        ag_y[e] = send(tok, X.at[land(e), 0, 0], ypeer(e))
    sib_own = send(tok, X.at[0, 0, 1], sibling)

    first_head = z * cz < H

    def head_taps(ref):
        both = ref[...].astype(F32)
        return jnp.where(first_head, both[0:1], both[1:2])

    for copy in taps:
        copy.wait()
    build_toeplitz(head_taps(F1v), M1)

    sib_x, sib_y, ag_a, ag_b = [], [], [], []
    for g, (lo, hi) in enumerate(groups):
        for e in range(1, q):
            if lo <= land(e) < hi:
                ag_x[e].wait_recv()
        ag_a.append(
            {e: send(X.at[0, lo:hi, 0, 0:H], X.at[land(e), lo:hi, 0, 0:H], ypeer(e)) for e in steps}
        )
        for e in range(1, q):
            if lo <= land(e) < hi:
                ag_y[e].wait_recv()
        ag_b.append(
            {e: send(X.at[lo:hi, 0, 0, H:B], X.at[lo:hi, land(e), 0, H:B], xpeer(e)) for e in steps}
        )
        sib_x.append(send(X.at[0, lo:hi, 0], X.at[0, lo:hi, 1], sibling))
        sib_y.append(send(X.at[lo:hi, 0, 0], X.at[lo:hi, 0, 1], sibling))
        if g == 0:
            build_toeplitz(head_taps(F2v), M2)

    def chip_of(dy, dx):
        return ((y + offsets[dy]) % q) * q + (x + offsets[dx]) % q

    def terms(dy, dx, lo, hi):
        tile = jnp.concatenate([X[dy, dx, 0], X[dy, dx, 1]], axis=1)
        c = chip_of(dy, dx)
        weight = jnp.concatenate([Wv[c, 0, :, lo:hi], Wv[c, 1, :, lo:hi]], axis=0)
        return jnp.dot(tile, weight, preferred_element_type=F32)

    def forward(g, e):
        lo, hi = groups[g]
        s = land(e)
        ag_a[g][e].wait_recv()
        a = send(X.at[s, lo:hi, 0, 0:H], X.at[s, lo:hi, 1, 0:H], sibling)
        ag_b[g][e].wait_recv()
        b = send(X.at[lo:hi, s, 0, H:B], X.at[lo:hi, s, 1, H:B], sibling)
        return [a, b]

    early = list(range(1, 1 + len(near)))
    late = list(range(1 + len(near), q))
    near_e = [e for e in range(1, q) if land(e) in early]
    far_e = [e for e in range(1, q) if land(e) in late]

    own.wait()
    for copy in weights:
        copy.wait()
    sib_own.wait_recv()
    total = terms(0, 0, 0, 3 * B)
    sib_x[0].wait_recv()
    sib_y[0].wait_recv()
    for d in early:
        total += terms(0, d, 0, 3 * B)
        total += terms(d, 0, 0, 3 * B)
    acc[...] = total
    first_fwd = []
    for e in near_e:
        first_fwd += forward(0, e)
    last_fwd = []
    for g, es in [(0, far_e)] + [(g, near_e + far_e) for g in range(1, len(groups))]:
        for e in es:
            last_fwd += forward(g, e)
    total = acc[...]
    for g in range(1, len(groups)):
        sib_x[g].wait_recv()
        sib_y[g].wait_recv()
        for d in range(*groups[g]):
            total += terms(0, d, 0, 3 * B)
            total += terms(d, 0, 0, 3 * B)
    for copy in first_fwd:
        copy.wait_recv()
    for dy in early:
        for dx in early:
            total += terms(dy, dx, 0, 3 * B)
    acc[...] = total
    for copy in last_fwd:
        copy.wait_recv()

    rest = [(dy, dx) for dy in range(1, q) for dx in range(1, q) if dy in late or dx in late]
    total = acc[:, 0:B]
    for dy, dx in rest:
        total += terms(dy, dx, 0, B)
    S0[...] = jnp.transpose(total).astype(BF16).reshape(nz, cz, B)
    a2a_value = [send(S0.at[(z + e) % nz], G0.at[z], zpeer(e)) for e in far_first]
    G0[z] = S0[z]
    total = acc[:, B : 3 * B]
    for dy, dx in rest:
        total += terms(dy, dx, B, 3 * B)
    for part in range(2):
        flipped = jnp.transpose(total[:, part * B : part * B + B])
        S1[:, part] = flipped.astype(BF16).reshape(nz, cz, B)
    a2a_gates = [send(S1.at[(z + e) % nz], G1.at[z], zpeer(e)) for e in far_first]
    G1[z] = S1[z]

    outw, wo_s = [], []
    for c in range(q * q):
        outw.append(
            local(wo.at[:, pl.ds(pl.multiple_of((2 * c + core) * B, B), B)], Wc.at[c, 0])
        )
        wo_s.append(
            send(
                wo.at[:, pl.ds(pl.multiple_of((2 * c + 1 - core) * B, B), B)],
                Wc.at[c, 1],
                sibling,
            )
        )

    def conv_block(P_ref, t):
        total = None
        for s in range(nz):
            if 0 <= t - s < blocks:
                term = P_ref[s * cz : s * cz + cz, (t - s) * B : (t - s) * B + B]
                total = term if total is None else total + term
        return total

    for copy in a2a_value:
        copy.wait_recv()
    signal = G0[...].reshape(B, B)
    P1[:, : prompt * B] = jnp.dot(signal, M1[:, : prompt * B], preferred_element_type=F32)
    for copy in a2a_gates:
        copy.wait_recv()
    for t in range(prompt):
        mixed = (G1[t, 0].astype(F32) * conv_block(P1, t)).astype(BF16)
        U2[t * cz : t * cz + cz, :] = mixed
    P2[:, : prompt * B] = jnp.dot(U2[...], M2[:, : prompt * B], preferred_element_type=F32)
    for t in range(prompt):
        S2[t] = (G1[t, 1].astype(F32) * conv_block(P2, t)).astype(BF16)
    back = {e: send(S2.at[(z + e) % nz], V.at[0, z], zpeer(e)) for e in far_first}
    fwd = [send(S2.at[z], V.at[1, z], sibling)]
    V[0, z] = S2[z]
    for sig, M_ref, P_ref, FS in ((signal, M1, P1, FS1), (U2[...], M2, P2, FS2)):
        P_ref[:, prompt * B :] = jnp.dot(sig, M_ref[:, prompt * B :], preferred_element_type=F32)
        for t in range(prompt, blocks):
            FS[t - prompt] = conv_block(P_ref, t)
    for copy in outw:
        copy.wait()
    for copy in wo_s:
        copy.wait_recv()
    for e in near_first:
        back[e].wait_recv()
        source = (z + nz - e) % nz
        fwd.append(send(V.at[0, source], V.at[1, source], sibling))
    for copy in fwd:
        copy.wait_recv()

    mixed = jnp.transpose(V[...].reshape(2 * B, B).astype(F32)).astype(BF16)

    def out_block(dy, dx):
        c = chip_of(dy, dx)
        weight = jnp.concatenate([Wc[c, 0], Wc[c, 1]], axis=0)
        block = jnp.dot(mixed, weight, preferred_element_type=F32)
        if dx == 0:
            OA[dy] = block[0:H]
        if dy == 0:
            OB[dx] = block[H:B]
        if dx or dy:
            PS[dy, dx] = block.astype(BF16)

    done = set()
    rs_a, rs_b = {}, {}
    for e in reversed(steps):
        s = slot_of[e]
        for d in range(q):
            for at in ((d, s), (s, d)):
                if at not in done:
                    done.add(at)
                    out_block(*at)
            if d == q - 1:
                rs_a[e] = send(PS.at[:, s, 0:H], RA.at[land(e)], xpeer(e))
                rs_b[e] = send(PS.at[s, :, H:B], RB.at[land(e)], ypeer(e))
    out_block(0, 0)

    future = []
    for FS, FL in ((FS1, FL1), (FS2, FL2)):
        future.append([send(FS.at[((z + e) % nz) // 2], FL.at[z], zpeer(e)) for e in far_first])
        FL[z] = FS[z // 2]

    def gather_sums(copies_in, O, R, Q):
        for copy in copies_in.values():
            copy.wait_recv()
        for d in range(q):
            total = O[d]
            for e in range(1, q):
                total += R[e, d].astype(F32)
            if d == 0:
                O[d] = total
            else:
                Q[d] = total.astype(BF16)

    gather_sums(rs_a, OA, RA, QA)
    rs_a2 = [send(QA.at[slot_of[e]], RA2.at[land(e)], ypeer(e)) for e in reversed(steps)]
    gather_sums(rs_b, OB, RB, QB)
    rs_b2 = [send(QB.at[slot_of[e]], RB2.at[land(e)], xpeer(e)) for e in reversed(steps)]

    for group, FL, ref in zip(future, (FL1, FL2), (ff, fs)):
        for copy in group:
            copy.wait_recv()
        rows = jnp.transpose(FL[...].reshape(B, B))
        ref[...] = jnp.where(z % 2 == 0, rows[0:H], rows[H:B])

    for group, O, R, rows in ((rs_a2, OA, RA2, slice(0, H)), (rs_b2, OB, RB2, slice(H, B))):
        for copy in group:
            copy.wait_recv()
        total = O[0]
        for e in range(1, q):
            total += R[e].astype(F32)
        out[rows, :] = total.astype(BF16)

    for copy in sent:
        copy.wait_send()
    assert counter[0] <= copies, counter[0]


def finish(a, b, c, out, ff, fs):
    out[...] = a[...]
    ff[...] = b[...]
    fs[...] = c[...]


def per_device(nz, tokens, input_weight, output_weight, filter_first, filter_second):
    depth, width = input_weight.shape[1:]
    chips = depth // (2 * B)
    q = int(round(chips**0.5))
    cz = B // nz
    taps = filter_first.shape[1]
    future = (taps // B - nz)
    copies = 160
    weights = input_weight.reshape(3, chips, 2, B, width)
    hbm = pl.BlockSpec(memory_space=pltpu.HBM)
    vmem = pl.BlockSpec(memory_space=pltpu.VMEM)
    scratch = [
        pltpu.VMEM((q, q, 2, B, B), BF16),
        pltpu.VMEM((chips, 2, B, 3 * B), BF16),
        pltpu.VMEM((chips, 2, B, B), BF16),
        pltpu.VMEM((B, 3 * B), F32),
        pltpu.VMEM((2, taps), BF16),
        pltpu.VMEM((2, taps), BF16),
        pltpu.VMEM((B, taps), BF16),
        pltpu.VMEM((B, taps), BF16),
        pltpu.VMEM((nz, cz, B), BF16),
        pltpu.VMEM((nz, 2, cz, B), BF16),
        pltpu.VMEM((nz, cz, B), BF16),
        pltpu.VMEM((nz, 2, cz, B), BF16),
        pltpu.VMEM((B, taps), F32),
        pltpu.VMEM((B, taps), F32),
        pltpu.VMEM((B, B), BF16),
        pltpu.VMEM((nz, cz, B), BF16),
        pltpu.VMEM((2, nz, cz, B), BF16),
        pltpu.VMEM((future, cz, B), F32),
        pltpu.VMEM((future, cz, B), F32),
        pltpu.VMEM((nz, cz, B), F32),
        pltpu.VMEM((nz, cz, B), F32),
        pltpu.VMEM((q, q, B, B), BF16),
        pltpu.VMEM((q, H, B), F32),
        pltpu.VMEM((q, H, B), F32),
        pltpu.VMEM((q, q, H, B), BF16),
        pltpu.VMEM((q, q, H, B), BF16),
        pltpu.VMEM((q, H, B), BF16),
        pltpu.VMEM((q, H, B), BF16),
        pltpu.VMEM((q, H, B), BF16),
        pltpu.VMEM((q, H, B), BF16),
        pltpu.SemaphoreType.DMA((copies,)),
        pltpu.SemaphoreType.DMA((copies,)),
        pltpu.SemaphoreType.DMA((9 + chips,)),
    ]
    operands = (tokens, weights, output_weight, filter_first, filter_second)
    operands = [pltpu.with_memory_space_constraint(a, pltpu.HBM) for a in operands]
    shapes = (
            jax.ShapeDtypeStruct((B, B), BF16),
            jax.ShapeDtypeStruct((H, B), F32),
            jax.ShapeDtypeStruct((H, B), F32),
        )
    parts = pl.pallas_call(
        functools.partial(kernel, q, nz, copies),
        out_shape=shapes,
        in_specs=[hbm] * 5,
        out_specs=(vmem, vmem, vmem),
        scratch_shapes=scratch,
        compiler_params=pltpu.CompilerParams(
            collective_id=0, has_side_effects=True, vmem_limit_bytes=32 * 2**20
        ),
    )(*operands)
    return pl.pallas_call(
        finish,
        out_shape=shapes,
        in_specs=[vmem] * 3,
        out_specs=(vmem, vmem, vmem),
        compiler_params=pltpu.CompilerParams(vmem_limit_bytes=2 * 2**20),
    )(*parts)


def solution(mesh):
    in_specs = (P("seq", "ch"), P(None, None, "ch"), P("ch", None), P("ch", None), P("ch", None))
    out_specs = (P("seq", "ch"), P("seq", "ch"), P("seq", "ch"))
    return jax.shard_map(
        functools.partial(per_device, mesh.shape["seq"]),
        mesh=mesh, in_specs=in_specs, out_specs=out_specs, check_vma=False,
    )
```

```python
import functools

import jax
import jax.numpy as jnp
from jax import lax
from jax.experimental import pallas as pl
from jax.experimental.pallas import tpu as pltpu
from jax.sharding import PartitionSpec as P

MESH = pl.DeviceIdType.MESH
B = 128
H = 64
F32 = jnp.float32
BF16 = jnp.bfloat16


def build_toeplitz(taps, matrix):
    width = taps.shape[1] + B
    padded = jnp.concatenate([jnp.zeros((1, B), F32), taps], axis=1)
    rows = jnp.broadcast_to(padded, (8, width))
    row = lax.broadcasted_iota(jnp.int32, (8, width), 0)
    for bit in (1, 2, 4):
        rows = jnp.where((row & bit) != 0, pltpu.roll(rows, bit, 1), rows)
    for pair in range(B // 16):
        low = rows if pair == 0 else pltpu.roll(rows, 16 * pair, 1)
        high = pltpu.roll(rows, 16 * pair + 8, 1)
        both = jnp.concatenate([low[:, B:], high[:, B:]], axis=0)
        matrix[16 * pair : 16 * pair + 16, :] = both.astype(BF16)


def kernel(
    q, nz, copies,
    tok, wi, wo, f1, f2,
    out, ff, fs,
    X, Wv, Wown, Wsib, acc, F1v, F2v, M1, M2, S0, S1, G0, G1, P1, P2, U2, S2, V,
    FS1, FS2, FL1, FL2, PS, OA, OB, RA, RB, QA, QB, RA2, RB2,
    ssem, rsem, lsem, plane_ready, column_ready,
):
    cz = B // nz
    prompt = nz
    blocks = M1.shape[1] // B
    z = lax.axis_index("seq")
    ch = lax.axis_index("ch")
    core = ch % 2
    x = (ch // 2) % q
    y = ch // (2 * q)

    near = [1, q - 1] if q > 2 else [1]
    offsets = [0] + near + [e for e in range(2, q - 1)]
    slot_of = {e: i for i, e in enumerate(offsets)}
    groups = [(1, 1 + len(near))] + [(i, i + 1) for i in range(1 + len(near), q)]
    steps = offsets[1:]

    def land(e):
        return slot_of[q - e]

    def ch_of(yy, xx, cc):
        return (yy * q + xx) * 2 + cc

    def xpeer(e):
        return (z, ch_of(y, (x + e) % q, core))

    def ypeer(e):
        return (z, ch_of((y + e) % q, x, core))

    sibling = (z, ch_of(y, x, 1 - core))

    def zpeer(e):
        return ((z + e) % nz, ch)

    far_first = sorted(range(1, nz), key=lambda e: -min(e, nz - e))
    near_first = sorted(range(1, nz), key=lambda e: min(e, nz - e))

    counter = [0]
    sent = []

    def send(src, dst, device):
        i = counter[0]
        counter[0] += 1
        copy = pltpu.make_async_remote_copy(
            src_ref=src, dst_ref=dst, send_sem=ssem.at[i], recv_sem=rsem.at[i],
            device_id=device, device_id_type=MESH,
        )
        copy.start()
        sent.append(copy)
        return copy

    local_count = [0]

    def local(src, dst):
        i = local_count[0]
        local_count[0] += 1
        copy = pltpu.make_async_copy(src, dst, lsem.at[i])
        copy.start()
        return copy

    barrier = pltpu.get_barrier_semaphore()

    def greet(device):
        pl.semaphore_signal(barrier, inc=1, device_id=device, device_id_type=MESH)

    for e in steps:
        greet((z, ch_of(y, (x + e) % q, 0)))
        greet((z, ch_of((y + e) % q, x, 0)))

    @pl.when(core == 1)
    def _():
        greet(sibling)

    for e in far_first:
        greet(((z + e) % nz, ch_of(y, x, 1)))

    own = local(tok, X.at[0, 0, 0])
    taps = [local(f1, F1v), local(f2, F2v)]
    weights = [local(wi.at[k], Wv.at[part]) for part, k in enumerate((2, 0, 1))]

    @pl.when(core == 0)
    def _():
        pl.semaphore_wait(barrier, 4 * (q - 1) + 1)
        pl.semaphore_signal(plane_ready, inc=1, device_id=sibling, device_id_type=MESH)

    @pl.when(core == 1)
    def _():
        pl.semaphore_wait(plane_ready, 1)


    ag_x, ag_y = {}, {}
    for e in steps:
        ag_x[e] = send(tok, X.at[0, land(e), 0], xpeer(e))
        ag_y[e] = send(tok, X.at[land(e), 0, 0], ypeer(e))
    sib_own = send(tok, X.at[0, 0, 1], sibling)

    first_head = z * cz < H

    def head_taps(ref):
        both = ref[...].astype(F32)
        return jnp.where(first_head, both[0:1], both[1:2])

    for copy in taps:
        copy.wait()
    build_toeplitz(head_taps(F1v), M1)

    sib_x, sib_y, ag_a, ag_b = [], [], [], []
    for g, (lo, hi) in enumerate(groups):
        for e in range(1, q):
            if lo <= land(e) < hi:
                ag_x[e].wait_recv()
        ag_a.append(
            {e: send(X.at[0, lo:hi, 0, 0:H], X.at[land(e), lo:hi, 0, 0:H], ypeer(e)) for e in steps}
        )
        for e in range(1, q):
            if lo <= land(e) < hi:
                ag_y[e].wait_recv()
        ag_b.append(
            {e: send(X.at[lo:hi, 0, 0, H:B], X.at[lo:hi, land(e), 0, H:B], xpeer(e)) for e in steps}
        )
        sib_x.append(send(X.at[0, lo:hi, 0], X.at[0, lo:hi, 1], sibling))
        sib_y.append(send(X.at[lo:hi, 0, 0], X.at[lo:hi, 0, 1], sibling))
        if g == 0:
            build_toeplitz(head_taps(F2v), M2)

    def chip_of(dy, dx):
        return ((y + offsets[dy]) % q) * q + (x + offsets[dx]) % q

    def terms(dy, dx, lo, hi):
        tile = jnp.concatenate([X[dy, dx, core], X[dy, dx, 1 - core]], axis=1)
        c = chip_of(dy, dx)
        weight = jnp.concatenate([Wv[part, c] for part in range(lo, hi)], axis=1)
        return jnp.dot(tile, weight, preferred_element_type=F32)

    def forward(g, e):
        lo, hi = groups[g]
        s = land(e)
        ag_a[g][e].wait_recv()
        a = send(X.at[s, lo:hi, 0, 0:H], X.at[s, lo:hi, 1, 0:H], sibling)
        ag_b[g][e].wait_recv()
        b = send(X.at[lo:hi, s, 0, H:B], X.at[lo:hi, s, 1, H:B], sibling)
        return [a, b]

    early = list(range(1, 1 + len(near)))
    late = list(range(1 + len(near), q))
    near_e = [e for e in range(1, q) if land(e) in early]
    far_e = [e for e in range(1, q) if land(e) in late]

    own.wait()
    for copy in weights:
        copy.wait()
    sib_own.wait_recv()
    total = terms(0, 0, 0, 3)
    sib_x[0].wait_recv()
    sib_y[0].wait_recv()
    for d in early:
        total += terms(0, d, 0, 3)
        total += terms(d, 0, 0, 3)
    acc[...] = total
    first_fwd = []
    for e in near_e:
        first_fwd += forward(0, e)
    last_fwd = []
    for g, es in [(0, far_e)] + [(g, near_e + far_e) for g in range(1, len(groups))]:
        for e in es:
            last_fwd += forward(g, e)

    @pl.when(core == 1)
    def _():
        pl.semaphore_wait(barrier, 2 * (nz - 1))
        pl.semaphore_signal(column_ready, inc=1, device_id=sibling, device_id_type=MESH)

    total = acc[...]
    for g in range(1, len(groups)):
        sib_x[g].wait_recv()
        sib_y[g].wait_recv()
        for d in range(*groups[g]):
            total += terms(0, d, 0, 3)
            total += terms(d, 0, 0, 3)
    for copy in first_fwd:
        copy.wait_recv()
    for dy in early:
        for dx in early:
            total += terms(dy, dx, 0, 3)
    acc[...] = total
    for copy in last_fwd:
        copy.wait_recv()

    @pl.when(core == 0)
    def _():
        pl.semaphore_wait(column_ready, 1)


    rest = [(dy, dx) for dy in range(1, q) for dx in range(1, q) if dy in late or dx in late]
    total = acc[:, 0:B]
    for dy, dx in rest:
        total += terms(dy, dx, 0, 1)
    S0[...] = jnp.transpose(total).astype(BF16).reshape(nz, cz, B)
    a2a_value = [send(S0.at[(z + e) % nz], G0.at[z], zpeer(e)) for e in far_first]
    G0[z] = S0[z]
    total = acc[:, B : 3 * B]
    for dy, dx in rest:
        total += terms(dy, dx, 1, 3)
    for part in range(2):
        flipped = jnp.transpose(total[:, part * B : part * B + B])
        S1[:, part] = flipped.astype(BF16).reshape(nz, cz, B)
    a2a_gates = [send(S1.at[(z + e) % nz], G1.at[z], zpeer(e)) for e in far_first]
    G1[z] = S1[z]

    outw = [local(wo, Wown)]
    wo_s = [send(wo, Wsib, sibling)]

    def conv_block(P_ref, t):
        total = None
        for s in range(nz):
            if 0 <= t - s < blocks:
                term = P_ref[s * cz : s * cz + cz, (t - s) * B : (t - s) * B + B]
                total = term if total is None else total + term
        return total

    for copy in a2a_value:
        copy.wait_recv()
    signal = G0[...].reshape(B, B)
    P1[:, : prompt * B] = jnp.dot(signal, M1[:, : prompt * B], preferred_element_type=F32)
    for copy in a2a_gates:
        copy.wait_recv()
    for t in range(prompt):
        mixed = (G1[t, 0].astype(F32) * conv_block(P1, t)).astype(BF16)
        U2[t * cz : t * cz + cz, :] = mixed
    P2[:, : prompt * B] = jnp.dot(U2[...], M2[:, : prompt * B], preferred_element_type=F32)
    for t in range(prompt):
        S2[t] = (G1[t, 1].astype(F32) * conv_block(P2, t)).astype(BF16)
    back = {e: send(S2.at[(z + e) % nz], V.at[0, z], zpeer(e)) for e in far_first}
    fwd = [send(S2.at[z], V.at[1, z], sibling)]
    V[0, z] = S2[z]
    for sig, M_ref, P_ref, FS in ((signal, M1, P1, FS1), (U2[...], M2, P2, FS2)):
        P_ref[:, prompt * B :] = jnp.dot(sig, M_ref[:, prompt * B :], preferred_element_type=F32)
        for t in range(prompt, blocks):
            FS[t - prompt] = conv_block(P_ref, t)
    for copy in outw:
        copy.wait()
    for copy in wo_s:
        copy.wait_recv()
    for e in near_first:
        back[e].wait_recv()
        source = (z + nz - e) % nz
        fwd.append(send(V.at[0, source], V.at[1, source], sibling))
    for copy in fwd:
        copy.wait_recv()

    mixed = jnp.transpose(V[...].reshape(2 * B, B).astype(F32)).astype(BF16)

    def out_block(dy, dx):
        c = chip_of(dy, dx)
        columns = pl.ds(pl.multiple_of((2 * c + core) * B, B), B)
        weight = jnp.concatenate([Wown[:, columns], Wsib[:, columns]], axis=0)
        block = jnp.dot(mixed, weight, preferred_element_type=F32)
        if dx == 0:
            OA[dy] = block[0:H]
        if dy == 0:
            OB[dx] = block[H:B]
        if dx or dy:
            PS[dy, dx] = block.astype(BF16)

    done = set()
    rs_a, rs_b = {}, {}
    for e in reversed(steps):
        s = slot_of[e]
        for d in range(q):
            for at in ((d, s), (s, d)):
                if at not in done:
                    done.add(at)
                    out_block(*at)
            if d == q - 1:
                rs_a[e] = send(PS.at[:, s, 0:H], RA.at[land(e)], xpeer(e))
                rs_b[e] = send(PS.at[s, :, H:B], RB.at[land(e)], ypeer(e))
    out_block(0, 0)

    future = []
    for FS, FL in ((FS1, FL1), (FS2, FL2)):
        future.append([send(FS.at[((z + e) % nz) // 2], FL.at[z], zpeer(e)) for e in far_first])
        FL[z] = FS[z // 2]

    def gather_sums(copies_in, O, R, Q):
        for copy in copies_in.values():
            copy.wait_recv()
        for d in range(q):
            total = O[d]
            for e in range(1, q):
                total += R[e, d].astype(F32)
            if d == 0:
                O[d] = total
            else:
                Q[d] = total.astype(BF16)

    gather_sums(rs_a, OA, RA, QA)
    rs_a2 = [send(QA.at[slot_of[e]], RA2.at[land(e)], ypeer(e)) for e in reversed(steps)]
    gather_sums(rs_b, OB, RB, QB)
    rs_b2 = [send(QB.at[slot_of[e]], RB2.at[land(e)], xpeer(e)) for e in reversed(steps)]

    for group, FL, ref in zip(future, (FL1, FL2), (ff, fs)):
        for copy in group:
            copy.wait_recv()
        rows = jnp.transpose(FL[...].reshape(B, B))
        ref[...] = jnp.where(z % 2 == 0, rows[0:H], rows[H:B])

    for group, O, R, rows in ((rs_a2, OA, RA2, slice(0, H)), (rs_b2, OB, RB2, slice(H, B))):
        for copy in group:
            copy.wait_recv()
        total = O[0]
        for e in range(1, q):
            total += R[e].astype(F32)
        out[rows, :] = total.astype(BF16)

    for copy in sent:
        copy.wait_send()
    assert counter[0] <= copies, counter[0]


def finish(a, b, c, out, ff, fs):
    out[...] = a[...]
    ff[...] = b[...]
    fs[...] = c[...]


def per_device(nz, tokens, input_weight, output_weight, filter_first, filter_second):
    depth, width = input_weight.shape[1:]
    chips = depth // (2 * B)
    q = int(round(chips**0.5))
    cz = B // nz
    taps = filter_first.shape[1]
    future = (taps // B - nz)
    copies = 160
    weights = input_weight.reshape(3, chips, 2 * B, width)
    hbm = pl.BlockSpec(memory_space=pltpu.HBM)
    vmem = pl.BlockSpec(memory_space=pltpu.VMEM)
    scratch = [
        pltpu.VMEM((q, q, 2, B, B), BF16),
        pltpu.VMEM((3, chips, 2 * B, B), BF16),
        pltpu.VMEM((B, 2 * chips * B), BF16),
        pltpu.VMEM((B, 2 * chips * B), BF16),
        pltpu.VMEM((B, 3 * B), F32),
        pltpu.VMEM((2, taps), BF16),
        pltpu.VMEM((2, taps), BF16),
        pltpu.VMEM((B, taps), BF16),
        pltpu.VMEM((B, taps), BF16),
        pltpu.VMEM((nz, cz, B), BF16),
        pltpu.VMEM((nz, 2, cz, B), BF16),
        pltpu.VMEM((nz, cz, B), BF16),
        pltpu.VMEM((nz, 2, cz, B), BF16),
        pltpu.VMEM((B, taps), F32),
        pltpu.VMEM((B, taps), F32),
        pltpu.VMEM((B, B), BF16),
        pltpu.VMEM((nz, cz, B), BF16),
        pltpu.VMEM((2, nz, cz, B), BF16),
        pltpu.VMEM((future, cz, B), F32),
        pltpu.VMEM((future, cz, B), F32),
        pltpu.VMEM((nz, cz, B), F32),
        pltpu.VMEM((nz, cz, B), F32),
        pltpu.VMEM((q, q, B, B), BF16),
        pltpu.VMEM((q, H, B), F32),
        pltpu.VMEM((q, H, B), F32),
        pltpu.VMEM((q, q, H, B), BF16),
        pltpu.VMEM((q, q, H, B), BF16),
        pltpu.VMEM((q, H, B), BF16),
        pltpu.VMEM((q, H, B), BF16),
        pltpu.VMEM((q, H, B), BF16),
        pltpu.VMEM((q, H, B), BF16),
        pltpu.SemaphoreType.DMA((copies,)),
        pltpu.SemaphoreType.DMA((copies,)),
        pltpu.SemaphoreType.DMA((8,)),
        pltpu.SemaphoreType.REGULAR,
        pltpu.SemaphoreType.REGULAR,
    ]
    operands = (tokens, weights, output_weight, filter_first, filter_second)
    operands = [pltpu.with_memory_space_constraint(a, pltpu.HBM) for a in operands]
    shapes = (
            jax.ShapeDtypeStruct((B, B), BF16),
            jax.ShapeDtypeStruct((H, B), F32),
            jax.ShapeDtypeStruct((H, B), F32),
        )
    parts = pl.pallas_call(
        functools.partial(kernel, q, nz, copies),
        out_shape=shapes,
        in_specs=[hbm] * 5,
        out_specs=(vmem, vmem, vmem),
        scratch_shapes=scratch,
        compiler_params=pltpu.CompilerParams(
            collective_id=0, has_side_effects=True, vmem_limit_bytes=32 * 2**20
        ),
    )(*operands)
    return pl.pallas_call(
        finish,
        out_shape=shapes,
        in_specs=[vmem] * 3,
        out_specs=(vmem, vmem, vmem),
        compiler_params=pltpu.CompilerParams(vmem_limit_bytes=2 * 2**20),
    )(*parts)


def solution(mesh):
    in_specs = (P("seq", "ch"), P(None, None, "ch"), P("ch", None), P("ch", None), P("ch", None))
    out_specs = (P("seq", "ch"), P("seq", "ch"), P("seq", "ch"))
    return jax.shard_map(
        functools.partial(per_device, mesh.shape["seq"]),
        mesh=mesh, in_specs=in_specs, out_specs=out_specs, check_vma=False,
    )
```

```python
import functools

import jax
import jax.numpy as jnp
from jax import lax
from jax.experimental import pallas as pl
from jax.experimental.pallas import tpu as pltpu
from jax.sharding import PartitionSpec as P

MESH = pl.DeviceIdType.MESH
B = 128
H = 64
F32 = jnp.float32
BF16 = jnp.bfloat16


def build_toeplitz(taps, matrix):
    width = taps.shape[1] + B
    padded = jnp.concatenate([jnp.zeros((1, B), F32), taps], axis=1)
    rows = jnp.broadcast_to(padded, (8, width))
    row = lax.broadcasted_iota(jnp.int32, (8, width), 0)
    for bit in (1, 2, 4):
        rows = jnp.where((row & bit) != 0, pltpu.roll(rows, bit, 1), rows)
    for pair in range(B // 16):
        low = rows if pair == 0 else pltpu.roll(rows, 16 * pair, 1)
        high = pltpu.roll(rows, 16 * pair + 8, 1)
        both = jnp.concatenate([low[:, B:], high[:, B:]], axis=0)
        matrix[16 * pair : 16 * pair + 16, :] = both.astype(BF16)


def kernel(
    q, nz, copies,
    tok, wi, wo, f1, f2,
    out, ff, fs,
    X, Wv, Wown, Wsib, acc, F, M1, M2, S0, S1, G0, G1, P1, P2, U2, S2, V,
    FS1, FS2, FL1, FL2, PS, OA, OB, RA, RB, QA, QB, RA2, RB2,
    ssem, rsem, lsem, plane_ready, column_ready,
):
    cz = B // nz
    prompt = nz
    blocks = M1.shape[1] // B
    z = lax.axis_index("seq")
    ch = lax.axis_index("ch")
    core = ch % 2
    x = (ch // 2) % q
    y = ch // (2 * q)

    near = [1, q - 1] if q > 2 else [1]
    offsets = [0] + near + [e for e in range(2, q - 1)]
    slot_of = {e: i for i, e in enumerate(offsets)}
    groups = [(1, 1 + len(near))] + [(i, i + 1) for i in range(1 + len(near), q)]
    steps = offsets[1:]

    def land(e):
        return slot_of[q - e]

    def ch_of(yy, xx, cc):
        return (yy * q + xx) * 2 + cc

    def xpeer(e):
        return (z, ch_of(y, (x + e) % q, core))

    def ypeer(e):
        return (z, ch_of((y + e) % q, x, core))

    sibling = (z, ch_of(y, x, 1 - core))

    def zpeer(e):
        return ((z + e) % nz, ch)

    far_first = sorted(range(1, nz), key=lambda e: -min(e, nz - e))
    near_first = sorted(range(1, nz), key=lambda e: min(e, nz - e))

    counts = {"send": 0, "receive": 0}
    sent = []

    def fresh(kind):
        counts[kind] += 1
        return counts[kind] - 1

    def transfer(src, dst, device, s, r):
        return pltpu.make_async_remote_copy(
            src_ref=src, dst_ref=dst, send_sem=ssem.at[s], recv_sem=rsem.at[r],
            device_id=device, device_id_type=MESH,
        )

    def out_of(ref):
        s = fresh("send")
        sent.append((ref, s))
        return s

    def send(src, dst, device, s, r):
        copy = transfer(src, dst, device, s, r)
        copy.start()
        return copy

    def landed(ref, r):
        transfer(ref, ref, sibling, 0, r).wait_recv()

    barrier = pltpu.get_barrier_semaphore()

    def greet(device):
        pl.semaphore_signal(barrier, inc=1, device_id=device, device_id_type=MESH)

    for e in steps:
        greet((z, ch_of(y, (x + e) % q, 0)))
        greet((z, ch_of((y + e) % q, x, 0)))

    @pl.when(core == 1)
    def _():
        greet(sibling)

    for e in far_first:
        greet(((z + e) % nz, ch_of(y, x, 1)))

    own = pltpu.make_async_copy(tok, X.at[0, 0, 0], lsem.at[0])
    own.start()
    for i, ref in enumerate((f1, f2)):
        pltpu.make_async_copy(ref, F.at[i], lsem.at[1]).start()
    for part, k in enumerate((2, 0, 1)):
        pltpu.make_async_copy(wi.at[k], Wv.at[part], lsem.at[2]).start()
    own.wait()

    @pl.when(core == 0)
    def _():
        pl.semaphore_wait(barrier, 4 * (q - 1) + 1)
        pl.semaphore_signal(plane_ready, inc=1, device_id=sibling, device_id_type=MESH)

    @pl.when(core == 1)
    def _():
        pl.semaphore_wait(plane_ready, 1)


    s = out_of(X.at[0, 0 : q - 1])
    ag_x = [fresh("receive") for _ in groups]
    ag_y = [fresh("receive") for _ in groups]

    def group_of(slot):
        return [lo <= slot < hi for lo, hi in groups].index(True)

    for e in steps:
        g = group_of(land(e))
        send(X.at[0, 0, 0], X.at[0, land(e), 0], xpeer(e), s, ag_x[g])
        send(X.at[0, 0, 0], X.at[land(e), 0, 0], ypeer(e), s, ag_y[g])
    sib_own = send(
        X.at[0, 0, 0], X.at[0, 0, 1], sibling, out_of(X.at[0, 0, 0]), fresh("receive")
    )

    first_head = z * cz < H

    def head_taps(i):
        both = F[i].astype(F32)
        return jnp.where(first_head, both[0:1], both[1:2])

    pltpu.make_async_copy(F, F, lsem.at[1]).wait()
    build_toeplitz(head_taps(0), M1)

    sib_xy, ag_a, ag_b = [], [], []
    for g, (lo, hi) in enumerate(groups):
        s = out_of(X.at[0 : hi - lo, 0 : q - 1, 0])
        landed(X.at[0, lo:hi, 0], ag_x[g])
        ag_a.append({
            e: send(
                X.at[0, lo:hi, 0, 0:H], X.at[land(e), lo:hi, 0, 0:H], ypeer(e), s, fresh("receive")
            )
            for e in steps
        })
        landed(X.at[lo:hi, 0, 0], ag_y[g])
        ag_b.append({
            e: send(
                X.at[lo:hi, 0, 0, H:B], X.at[lo:hi, land(e), 0, H:B], xpeer(e), s, fresh("receive")
            )
            for e in steps
        })
        s, r = out_of(X.at[0, lo:hi]), fresh("receive")
        send(X.at[0, lo:hi, 0], X.at[0, lo:hi, 1], sibling, s, r)
        send(X.at[lo:hi, 0, 0], X.at[lo:hi, 0, 1], sibling, s, r)
        sib_xy.append(r)
        if g == 0:
            build_toeplitz(head_taps(1), M2)

    def chip_of(dy, dx):
        return ((y + offsets[dy]) % q) * q + (x + offsets[dx]) % q

    def terms(dy, dx, lo, hi):
        tile = jnp.concatenate([X[dy, dx, core], X[dy, dx, 1 - core]], axis=1)
        c = chip_of(dy, dx)
        weight = jnp.concatenate([Wv[part, c] for part in range(lo, hi)], axis=1)
        return jnp.dot(tile, weight, preferred_element_type=F32)

    def forward(g, e, s, r):
        lo, hi = groups[g]
        at = land(e)
        ag_a[g][e].wait_recv()
        send(X.at[at, lo:hi, 0, 0:H], X.at[at, lo:hi, 1, 0:H], sibling, s, r)
        ag_b[g][e].wait_recv()
        send(X.at[lo:hi, at, 0, H:B], X.at[lo:hi, at, 1, H:B], sibling, s, r)

    early = list(range(1, 1 + len(near)))
    late = list(range(1 + len(near), q))
    near_e = [e for e in range(1, q) if land(e) in early]
    far_e = [e for e in range(1, q) if land(e) in late]

    pltpu.make_async_copy(Wv, Wv, lsem.at[2]).wait()
    sib_own.wait_recv()
    total = terms(0, 0, 0, 3)
    landed(X.at[0, 1 : 1 + len(near)], sib_xy[0])
    for d in early:
        total += terms(0, d, 0, 3)
        total += terms(d, 0, 0, 3)
    acc[...] = total
    corner = X.at[1 : 1 + len(near), 1 : 1 + len(near), 1]
    s, first_fwd = out_of(corner), fresh("receive")
    for e in near_e:
        forward(0, e, s, first_fwd)
    last_fwd = []
    if far_e:
        ref = X.at[1 + len(near) : q, 1 : 1 + len(near), 1]
        s, r = out_of(ref), fresh("receive")
        last_fwd.append((ref, r))
        for e in far_e:
            forward(0, e, s, r)
    for g in range(1, len(groups)):
        lo, hi = groups[g]
        ref = X.at[lo:hi, 1:q, 1]
        s, r = out_of(ref), fresh("receive")
        last_fwd.append((ref, r))
        for e in near_e + far_e:
            forward(g, e, s, r)

    @pl.when(core == 1)
    def _():
        pl.semaphore_wait(barrier, 2 * (nz - 1))
        pl.semaphore_signal(column_ready, inc=1, device_id=sibling, device_id_type=MESH)

    total = acc[...]
    for g in range(1, len(groups)):
        landed(X.at[0, groups[g][0] : groups[g][1]], sib_xy[g])
        for d in range(*groups[g]):
            total += terms(0, d, 0, 3)
            total += terms(d, 0, 0, 3)
    landed(corner, first_fwd)
    for dy in early:
        for dx in early:
            total += terms(dy, dx, 0, 3)
    acc[...] = total
    for ref, r in last_fwd:
        landed(ref, r)

    @pl.when(core == 0)
    def _():
        pl.semaphore_wait(column_ready, 1)


    rest = [(dy, dx) for dy in range(1, q) for dx in range(1, q) if dy in late or dx in late]
    total = acc[:, 0:B]
    for dy, dx in rest:
        total += terms(dy, dx, 0, 1)
    S0[...] = jnp.transpose(total).astype(BF16).reshape(nz, cz, B)
    s, value_in = out_of(S0.at[0 : nz - 1]), fresh("receive")
    for e in far_first:
        send(S0.at[(z + e) % nz], G0.at[z], zpeer(e), s, value_in)
    G0[z] = S0[z]
    total = acc[:, B : 3 * B]
    for dy, dx in rest:
        total += terms(dy, dx, 1, 3)
    for part in range(2):
        flipped = jnp.transpose(total[:, part * B : part * B + B])
        S1[:, part] = flipped.astype(BF16).reshape(nz, cz, B)
    s, gates_in = out_of(S1.at[0 : nz - 1]), fresh("receive")
    for e in far_first:
        send(S1.at[(z + e) % nz], G1.at[z], zpeer(e), s, gates_in)
    G1[z] = S1[z]

    own_rows = pltpu.make_async_copy(wo, Wown, lsem.at[3])
    own_rows.start()
    sibling_rows = send(wo, Wsib, sibling, out_of(Wsib), fresh("receive"))

    def conv_block(P_ref, t):
        total = None
        for s in range(nz):
            if 0 <= t - s < blocks:
                term = P_ref[s * cz : s * cz + cz, (t - s) * B : (t - s) * B + B]
                total = term if total is None else total + term
        return total

    landed(G0.at[0 : nz - 1], value_in)
    signal = G0[...].reshape(B, B)
    P1[:, : prompt * B] = jnp.dot(signal, M1[:, : prompt * B], preferred_element_type=F32)
    landed(G1.at[0 : nz - 1], gates_in)
    for t in range(prompt):
        mixed = (G1[t, 0].astype(F32) * conv_block(P1, t)).astype(BF16)
        U2[t * cz : t * cz + cz, :] = mixed
    P2[:, : prompt * B] = jnp.dot(U2[...], M2[:, : prompt * B], preferred_element_type=F32)
    for t in range(prompt):
        S2[t] = (G1[t, 1].astype(F32) * conv_block(P2, t)).astype(BF16)
    s = out_of(S2.at[0 : nz - 1])
    back = {
        e: send(S2.at[(z + e) % nz], V.at[0, z], zpeer(e), s, fresh("receive")) for e in far_first
    }
    s, fwd = out_of(V.at[1]), fresh("receive")
    send(S2.at[z], V.at[1, z], sibling, s, fwd)
    V[0, z] = S2[z]
    for sig, M_ref, P_ref, FS in ((signal, M1, P1, FS1), (U2[...], M2, P2, FS2)):
        P_ref[:, prompt * B :] = jnp.dot(sig, M_ref[:, prompt * B :], preferred_element_type=F32)
        for t in range(prompt, blocks):
            FS[t - prompt] = conv_block(P_ref, t)
    own_rows.wait()
    sibling_rows.wait_recv()
    for e in near_first:
        back[e].wait_recv()
        source = (z + nz - e) % nz
        send(V.at[0, source], V.at[1, source], sibling, s, fwd)
    landed(V.at[1], fwd)

    mixed = jnp.transpose(V[...].reshape(2 * B, B).astype(F32)).astype(BF16)

    def out_block(dy, dx):
        c = chip_of(dy, dx)
        columns = pl.ds(pl.multiple_of((2 * c + core) * B, B), B)
        weight = jnp.concatenate([Wown[:, columns], Wsib[:, columns]], axis=0)
        block = jnp.dot(mixed, weight, preferred_element_type=F32)
        if dx == 0:
            OA[dy] = block[0:H]
        if dy == 0:
            OB[dx] = block[H:B]
        if dx or dy:
            PS[dy, dx] = block.astype(BF16)

    done = set()
    (sa, rs_a), (sb, rs_b) = ((out_of(R.at[1:q]), fresh("receive")) for R in (RA, RB))
    for e in reversed(steps):
        s = slot_of[e]
        for d in range(q):
            for at in ((d, s), (s, d)):
                if at not in done:
                    done.add(at)
                    out_block(*at)
            if d == q - 1:
                send(PS.at[:, s, 0:H], RA.at[land(e)], xpeer(e), sa, rs_a)
                send(PS.at[s, :, H:B], RB.at[land(e)], ypeer(e), sb, rs_b)
    out_block(0, 0)

    future = []
    for FS, FL in ((FS1, FL1), (FS2, FL2)):
        s, r = out_of(FL.at[0 : nz - 1]), fresh("receive")
        for e in far_first:
            send(FS.at[((z + e) % nz) // 2], FL.at[z], zpeer(e), s, r)
        future.append(r)
        FL[z] = FS[z // 2]

    def gather_sums(r, O, R, Q):
        landed(R.at[1:q], r)
        for d in range(q):
            total = O[d]
            for e in range(1, q):
                total += R[e, d].astype(F32)
            if d == 0:
                O[d] = total
            else:
                Q[d] = total.astype(BF16)

    gather_sums(rs_a, OA, RA, QA)
    s, rs_a2 = out_of(RA2.at[1:q]), fresh("receive")
    for e in reversed(steps):
        send(QA.at[slot_of[e]], RA2.at[land(e)], ypeer(e), s, rs_a2)
    gather_sums(rs_b, OB, RB, QB)
    s, rs_b2 = out_of(RB2.at[1:q]), fresh("receive")
    for e in reversed(steps):
        send(QB.at[slot_of[e]], RB2.at[land(e)], xpeer(e), s, rs_b2)

    for r, FL, ref in zip(future, (FL1, FL2), (ff, fs)):
        landed(FL.at[0 : nz - 1], r)
        rows = jnp.transpose(FL[...].reshape(B, B))
        ref[...] = jnp.where(z % 2 == 0, rows[0:H], rows[H:B])

    for r, O, R, rows in ((rs_a2, OA, RA2, slice(0, H)), (rs_b2, OB, RB2, slice(H, B))):
        landed(R.at[1:q], r)
        total = O[0]
        for e in range(1, q):
            total += R[e].astype(F32)
        out[rows, :] = total.astype(BF16)

    for ref, s in sent:
        transfer(ref, ref, sibling, s, 0).wait_send()
    assert counts == {"send": copies[0], "receive": copies[1]}, counts


def finish(a, b, c, out, ff, fs):
    out[...] = a[...]
    ff[...] = b[...]
    fs[...] = c[...]


def per_device(nz, tokens, input_weight, output_weight, filter_first, filter_second):
    depth, width = input_weight.shape[1:]
    chips = depth // (2 * B)
    q = int(round(chips**0.5))
    cz = B // nz
    taps = filter_first.shape[1]
    future = (taps // B - nz)
    groups = 2 if q > 2 else 1
    copies = (
        1 + 1 + 2 * groups + 1 + (2 * groups - 2) + 11,
        2 * groups + 1 + 2 * groups * (q - 1) + groups + 1 + (2 * groups - 2) + 3 + nz + 6,
    )
    weights = input_weight.reshape(3, chips, 2 * B, width)
    hbm = pl.BlockSpec(memory_space=pltpu.HBM)
    vmem = pl.BlockSpec(memory_space=pltpu.VMEM)
    scratch = [
        pltpu.VMEM((q, q, 2, B, B), BF16),
        pltpu.VMEM((3, chips, 2 * B, B), BF16),
        pltpu.VMEM((B, 2 * chips * B), BF16),
        pltpu.VMEM((B, 2 * chips * B), BF16),
        pltpu.VMEM((B, 3 * B), F32),
        pltpu.VMEM((2, 2, taps), BF16),
        pltpu.VMEM((B, taps), BF16),
        pltpu.VMEM((B, taps), BF16),
        pltpu.VMEM((nz, cz, B), BF16),
        pltpu.VMEM((nz, 2, cz, B), BF16),
        pltpu.VMEM((nz, cz, B), BF16),
        pltpu.VMEM((nz, 2, cz, B), BF16),
        pltpu.VMEM((B, taps), F32),
        pltpu.VMEM((B, taps), F32),
        pltpu.VMEM((B, B), BF16),
        pltpu.VMEM((nz, cz, B), BF16),
        pltpu.VMEM((2, nz, cz, B), BF16),
        pltpu.VMEM((future, cz, B), F32),
        pltpu.VMEM((future, cz, B), F32),
        pltpu.VMEM((nz, cz, B), F32),
        pltpu.VMEM((nz, cz, B), F32),
        pltpu.VMEM((q, q, B, B), BF16),
        pltpu.VMEM((q, H, B), F32),
        pltpu.VMEM((q, H, B), F32),
        pltpu.VMEM((q, q, H, B), BF16),
        pltpu.VMEM((q, q, H, B), BF16),
        pltpu.VMEM((q, H, B), BF16),
        pltpu.VMEM((q, H, B), BF16),
        pltpu.VMEM((q, H, B), BF16),
        pltpu.VMEM((q, H, B), BF16),
        pltpu.SemaphoreType.DMA((copies[0],)),
        pltpu.SemaphoreType.DMA((copies[1],)),
        pltpu.SemaphoreType.DMA((4,)),
        pltpu.SemaphoreType.REGULAR,
        pltpu.SemaphoreType.REGULAR,
    ]
    operands = (tokens, weights, output_weight, filter_first, filter_second)
    operands = [pltpu.with_memory_space_constraint(a, pltpu.HBM) for a in operands]
    shapes = (
            jax.ShapeDtypeStruct((B, B), BF16),
            jax.ShapeDtypeStruct((H, B), F32),
            jax.ShapeDtypeStruct((H, B), F32),
        )
    parts = pl.pallas_call(
        functools.partial(kernel, q, nz, copies),
        out_shape=shapes,
        in_specs=[hbm] * 5,
        out_specs=(vmem, vmem, vmem),
        scratch_shapes=scratch,
        compiler_params=pltpu.CompilerParams(
            collective_id=0, has_side_effects=True, vmem_limit_bytes=32 * 2**20
        ),
    )(*operands)
    return pl.pallas_call(
        finish,
        out_shape=shapes,
        in_specs=[vmem] * 3,
        out_specs=(vmem, vmem, vmem),
        compiler_params=pltpu.CompilerParams(vmem_limit_bytes=2 * 2**20),
    )(*parts)


def solution(mesh):
    in_specs = (P("seq", "ch"), P(None, None, "ch"), P("ch", None), P("ch", None), P("ch", None))
    out_specs = (P("seq", "ch"), P("seq", "ch"), P("seq", "ch"))
    return jax.shard_map(
        functools.partial(per_device, mesh.shape["seq"]),
        mesh=mesh, in_specs=in_specs, out_specs=out_specs, check_vma=False,
    )
```

```python
import functools

import jax
import jax.numpy as jnp
from jax import lax
from jax.experimental import pallas as pl
from jax.experimental.pallas import tpu as pltpu
from jax.sharding import PartitionSpec as P

MESH = pl.DeviceIdType.MESH
B = 128
H = 64
F32 = jnp.float32
BF16 = jnp.bfloat16


def build_toeplitz(taps, matrix):
    width = taps.shape[1] + B
    padded = jnp.concatenate([jnp.zeros((1, B), F32), taps], axis=1)
    rows = jnp.broadcast_to(padded, (8, width))
    row = lax.broadcasted_iota(jnp.int32, (8, width), 0)
    for bit in (1, 2, 4):
        rows = jnp.where((row & bit) != 0, pltpu.roll(rows, bit, 1), rows)
    for pair in range(B // 16):
        low = rows if pair == 0 else pltpu.roll(rows, 16 * pair, 1)
        high = pltpu.roll(rows, 16 * pair + 8, 1)
        both = jnp.concatenate([low[:, B:], high[:, B:]], axis=0)
        matrix[16 * pair : 16 * pair + 16, :] = both.astype(BF16)


def kernel(
    q, nz, copies,
    tok, wi, wo, f1, f2,
    out, ff, fs,
    X, Wv, Wown, Wsib, acc, F, M1, M2, S0, S1, G0, G1, P1, P2, U2, S2, V,
    FS1, FS2, FL1, FL2, PS, OA, OB, RA, RB, QA, QB, RA2, RB2,
    ssem, rsem, lsem, plane_ready, column_ready,
):
    cz = B // nz
    prompt = nz
    blocks = M1.shape[1] // B
    z = lax.axis_index("seq")
    ch = lax.axis_index("ch")
    core = ch % 2
    x = (ch // 2) % q
    y = ch // (2 * q)

    near = [1, q - 1] if q > 2 else [1]
    offsets = [0] + near + [e for e in range(2, q - 1)]
    slot_of = {e: i for i, e in enumerate(offsets)}
    groups = [(1, 1 + len(near))] + [(i, i + 1) for i in range(1 + len(near), q)]
    steps = offsets[1:]

    def land(e):
        return slot_of[q - e]

    def ch_of(yy, xx, cc):
        return (yy * q + xx) * 2 + cc

    def xpeer(e):
        return (z, ch_of(y, (x + e) % q, core))

    def ypeer(e):
        return (z, ch_of((y + e) % q, x, core))

    sibling = (z, ch_of(y, x, 1 - core))

    def zpeer(e):
        return ((z + e) % nz, ch)

    far_first = sorted(range(1, nz), key=lambda e: -min(e, nz - e))
    near_first = sorted(range(1, nz), key=lambda e: min(e, nz - e))

    counts = {"send": 0, "receive": 0}
    sent = []

    def fresh(kind):
        counts[kind] += 1
        return counts[kind] - 1

    def transfer(src, dst, device, s, r):
        return pltpu.make_async_remote_copy(
            src_ref=src, dst_ref=dst, send_sem=ssem.at[s], recv_sem=rsem.at[r],
            device_id=device, device_id_type=MESH,
        )

    def out_of(ref):
        s = fresh("send")
        sent.append((ref, s))
        return s

    def send(src, dst, device, s, r):
        copy = transfer(src, dst, device, s, r)
        copy.start()
        return copy

    def landed(ref, r):
        transfer(ref, ref, sibling, 0, r).wait_recv()

    barrier = pltpu.get_barrier_semaphore()

    def greet(device):
        pl.semaphore_signal(barrier, inc=1, device_id=device, device_id_type=MESH)

    for e in steps:
        greet((z, ch_of(y, (x + e) % q, 0)))
        greet((z, ch_of((y + e) % q, x, 0)))

    @pl.when(core == 1)
    def _():
        greet(sibling)

    for e in far_first:
        greet(((z + e) % nz, ch_of(y, x, 1)))

    own = pltpu.make_async_copy(tok, X.at[0, 0, 0], lsem.at[0])
    own.start()
    for i, ref in enumerate((f1, f2)):
        pltpu.make_async_copy(ref, F.at[i], lsem.at[1]).start()
    for part, k in enumerate((2, 0, 1)):
        pltpu.make_async_copy(wi.at[k], Wv.at[part], lsem.at[2]).start()
    own.wait()

    @pl.when(core == 0)
    def _():
        pl.semaphore_wait(barrier, 4 * (q - 1) + 1)
        pl.semaphore_signal(plane_ready, inc=1, device_id=sibling, device_id_type=MESH)

    @pl.when(core == 1)
    def _():
        pl.semaphore_wait(plane_ready, 1)


    s = out_of(X.at[0, 0 : q - 1])
    ag_x = [fresh("receive") for _ in groups]
    ag_y = [fresh("receive") for _ in groups]

    def group_of(slot):
        return [lo <= slot < hi for lo, hi in groups].index(True)

    for e in steps:
        g = group_of(land(e))
        send(X.at[0, 0, 0], X.at[0, land(e), 0], xpeer(e), s, ag_x[g])
        send(X.at[0, 0, 0], X.at[land(e), 0, 0], ypeer(e), s, ag_y[g])
    sib_own = send(
        X.at[0, 0, 0], X.at[0, 0, 1], sibling, out_of(X.at[0, 0, 0]), fresh("receive")
    )

    first_head = z * cz < H

    def head_taps(i):
        both = F[i].astype(F32)
        return jnp.where(first_head, both[0:1], both[1:2])

    pltpu.make_async_copy(F, F, lsem.at[1]).wait()
    build_toeplitz(head_taps(0), M1)

    sib_xy, ag_a, ag_b = [], [], []
    for g, (lo, hi) in enumerate(groups):
        s = out_of(X.at[0 : hi - lo, 0 : q - 1, 0])
        landed(X.at[0, lo:hi, 0], ag_x[g])
        ag_a.append({
            e: send(
                X.at[0, lo:hi, 0, 0:H], X.at[land(e), lo:hi, 0, 0:H], ypeer(e), s, fresh("receive")
            )
            for e in steps
        })
        landed(X.at[lo:hi, 0, 0], ag_y[g])
        ag_b.append({
            e: send(
                X.at[lo:hi, 0, 0, H:B], X.at[lo:hi, land(e), 0, H:B], xpeer(e), s, fresh("receive")
            )
            for e in steps
        })
        s, r = out_of(X.at[0, lo:hi]), fresh("receive")
        send(X.at[0, lo:hi, 0], X.at[0, lo:hi, 1], sibling, s, r)
        send(X.at[lo:hi, 0, 0], X.at[lo:hi, 0, 1], sibling, s, r)
        sib_xy.append(r)
        if g == 0:
            build_toeplitz(head_taps(1), M2)

    def chip_of(dy, dx):
        return ((y + offsets[dy]) % q) * q + (x + offsets[dx]) % q

    def terms(dy, dx, lo, hi):
        tile = jnp.concatenate([X[dy, dx, core], X[dy, dx, 1 - core]], axis=1)
        c = chip_of(dy, dx)
        weight = jnp.concatenate([Wv[part, c] for part in range(lo, hi)], axis=1)
        return jnp.dot(tile, weight, preferred_element_type=F32)

    def forward(g, e, s, r):
        lo, hi = groups[g]
        at = land(e)
        ag_a[g][e].wait_recv()
        send(X.at[at, lo:hi, 0, 0:H], X.at[at, lo:hi, 1, 0:H], sibling, s, r)
        ag_b[g][e].wait_recv()
        send(X.at[lo:hi, at, 0, H:B], X.at[lo:hi, at, 1, H:B], sibling, s, r)

    early = list(range(1, 1 + len(near)))
    late = list(range(1 + len(near), q))
    near_e = [e for e in range(1, q) if land(e) in early]
    far_e = [e for e in range(1, q) if land(e) in late]

    pltpu.make_async_copy(Wv, Wv, lsem.at[2]).wait()
    sib_own.wait_recv()
    total = terms(0, 0, 0, 3)
    landed(X.at[0, 1 : 1 + len(near)], sib_xy[0])
    for d in early:
        total += terms(0, d, 0, 3)
        total += terms(d, 0, 0, 3)
    acc[...] = total
    corner = X.at[1 : 1 + len(near), 1 : 1 + len(near), 1]
    s, first_fwd = out_of(corner), fresh("receive")
    for e in near_e:
        forward(0, e, s, first_fwd)
    last_fwd = []
    if far_e:
        ref = X.at[1 + len(near) : q, 1 : 1 + len(near), 1]
        s, r = out_of(ref), fresh("receive")
        last_fwd.append((ref, r))
        for e in far_e:
            forward(0, e, s, r)
    for g in range(1, len(groups)):
        lo, hi = groups[g]
        ref = X.at[lo:hi, 1:q, 1]
        s, r = out_of(ref), fresh("receive")
        last_fwd.append((ref, r))
        for e in near_e + far_e:
            forward(g, e, s, r)

    @pl.when(core == 1)
    def _():
        pl.semaphore_wait(barrier, 2 * (nz - 1))
        pl.semaphore_signal(column_ready, inc=1, device_id=sibling, device_id_type=MESH)

    total = acc[...]
    for g in range(1, len(groups)):
        landed(X.at[0, groups[g][0] : groups[g][1]], sib_xy[g])
        for d in range(*groups[g]):
            total += terms(0, d, 0, 3)
            total += terms(d, 0, 0, 3)
    landed(corner, first_fwd)
    for dy in early:
        for dx in early:
            total += terms(dy, dx, 0, 3)
    acc[...] = total
    for ref, r in last_fwd:
        landed(ref, r)

    @pl.when(core == 0)
    def _():
        pl.semaphore_wait(column_ready, 1)


    rest = [(dy, dx) for dy in range(1, q) for dx in range(1, q) if dy in late or dx in late]
    total = acc[:, 0:B]
    for dy, dx in rest:
        total += terms(dy, dx, 0, 1)
    S0[...] = jnp.transpose(total).astype(BF16).reshape(nz, cz, B)
    s, value_in = out_of(S0.at[0 : nz - 1]), fresh("receive")
    for e in far_first:
        send(S0.at[(z + e) % nz], G0.at[z], zpeer(e), s, value_in)
    G0[z] = S0[z]
    gates_in = []
    for part in range(2):
        total = acc[:, part * B + B : part * B + 2 * B]
        for dy, dx in rest:
            total += terms(dy, dx, part + 1, part + 2)
        S1[part] = jnp.transpose(total).astype(BF16).reshape(nz, cz, B)
        s, r = out_of(S1.at[part, 0 : nz - 1]), fresh("receive")
        for e in far_first:
            send(S1.at[part, (z + e) % nz], G1.at[part, z], zpeer(e), s, r)
        G1[part, z] = S1[part, z]
        gates_in.append(r)

    own_rows = pltpu.make_async_copy(wo, Wown, lsem.at[3])
    own_rows.start()
    sibling_rows = send(wo, Wsib, sibling, out_of(Wsib), fresh("receive"))

    def conv_block(P_ref, t):
        total = None
        for s in range(nz):
            if 0 <= t - s < blocks:
                term = P_ref[s * cz : s * cz + cz, (t - s) * B : (t - s) * B + B]
                total = term if total is None else total + term
        return total

    landed(G0.at[0 : nz - 1], value_in)
    signal = G0[...].reshape(B, B)
    P1[:, : prompt * B] = jnp.dot(signal, M1[:, : prompt * B], preferred_element_type=F32)
    landed(G1.at[0, 0 : nz - 1], gates_in[0])
    for t in range(prompt):
        mixed = (G1[0, t].astype(F32) * conv_block(P1, t)).astype(BF16)
        U2[t * cz : t * cz + cz, :] = mixed
    P2[:, : prompt * B] = jnp.dot(U2[...], M2[:, : prompt * B], preferred_element_type=F32)
    landed(G1.at[1, 0 : nz - 1], gates_in[1])
    for t in range(prompt):
        S2[t] = (G1[1, t].astype(F32) * conv_block(P2, t)).astype(BF16)
    s = out_of(S2.at[0 : nz - 1])
    back = {
        e: send(S2.at[(z + e) % nz], V.at[0, z], zpeer(e), s, fresh("receive")) for e in far_first
    }
    s, fwd = out_of(V.at[1]), fresh("receive")
    send(S2.at[z], V.at[1, z], sibling, s, fwd)
    V[0, z] = S2[z]
    for sig, M_ref, P_ref, FS in ((signal, M1, P1, FS1), (U2[...], M2, P2, FS2)):
        P_ref[:, prompt * B :] = jnp.dot(sig, M_ref[:, prompt * B :], preferred_element_type=F32)
        for t in range(prompt, blocks):
            FS[t - prompt] = conv_block(P_ref, t)
    own_rows.wait()
    sibling_rows.wait_recv()
    for e in near_first:
        back[e].wait_recv()
        source = (z + nz - e) % nz
        send(V.at[0, source], V.at[1, source], sibling, s, fwd)
    own_half = jnp.transpose(V[0].reshape(B, B).astype(F32)).astype(BF16)
    landed(V.at[1], fwd)

    other_half = jnp.transpose(V[1].reshape(B, B).astype(F32)).astype(BF16)
    mixed = jnp.concatenate([own_half, other_half], axis=1)

    def out_block(dy, dx):
        c = chip_of(dy, dx)
        columns = pl.ds(pl.multiple_of((2 * c + core) * B, B), B)
        weight = jnp.concatenate([Wown[:, columns], Wsib[:, columns]], axis=0)
        block = jnp.dot(mixed, weight, preferred_element_type=F32)
        if dx == 0:
            OA[dy] = block[0:H]
        if dy == 0:
            OB[dx] = block[H:B]
        if dx or dy:
            PS[dy, dx] = block.astype(BF16)

    done = set()
    (sa, rs_a), (sb, rs_b) = ((out_of(R.at[1:q]), fresh("receive")) for R in (RA, RB))
    for e in reversed(steps):
        s = slot_of[e]
        for d in range(q):
            for at in ((d, s), (s, d)):
                if at not in done:
                    done.add(at)
                    out_block(*at)
            if d == q - 1:
                send(PS.at[:, s, 0:H], RA.at[land(e)], xpeer(e), sa, rs_a)
                send(PS.at[s, :, H:B], RB.at[land(e)], ypeer(e), sb, rs_b)
    out_block(0, 0)

    future = []
    for FS, FL in ((FS1, FL1), (FS2, FL2)):
        s, r = out_of(FL.at[0 : nz - 1]), fresh("receive")
        for e in far_first:
            send(FS.at[((z + e) % nz) // 2], FL.at[z], zpeer(e), s, r)
        future.append(r)
        FL[z] = FS[z // 2]

    def gather_sums(r, O, R, Q):
        landed(R.at[1:q], r)
        for d in range(q):
            total = O[d]
            for e in range(1, q):
                total += R[e, d].astype(F32)
            if d == 0:
                O[d] = total
            else:
                Q[d] = total.astype(BF16)

    gather_sums(rs_a, OA, RA, QA)
    s, rs_a2 = out_of(RA2.at[1:q]), fresh("receive")
    for e in reversed(steps):
        send(QA.at[slot_of[e]], RA2.at[land(e)], ypeer(e), s, rs_a2)
    gather_sums(rs_b, OB, RB, QB)
    s, rs_b2 = out_of(RB2.at[1:q]), fresh("receive")
    for e in reversed(steps):
        send(QB.at[slot_of[e]], RB2.at[land(e)], xpeer(e), s, rs_b2)

    for r, FL, ref in zip(future, (FL1, FL2), (ff, fs)):
        landed(FL.at[0 : nz - 1], r)
        rows = jnp.transpose(FL[...].reshape(B, B))
        ref[...] = jnp.where(z % 2 == 0, rows[0:H], rows[H:B])

    for r, O, R, rows in ((rs_a2, OA, RA2, slice(0, H)), (rs_b2, OB, RB2, slice(H, B))):
        landed(R.at[1:q], r)
        total = O[0]
        for e in range(1, q):
            total += R[e].astype(F32)
        out[rows, :] = total.astype(BF16)

    for ref, s in sent:
        transfer(ref, ref, sibling, s, 0).wait_send()
    assert counts == {"send": copies[0], "receive": copies[1]}, counts


def finish(a, b, c, out, ff, fs):
    out[...] = a[...]
    ff[...] = b[...]
    fs[...] = c[...]


def per_device(nz, tokens, input_weight, output_weight, filter_first, filter_second):
    depth, width = input_weight.shape[1:]
    chips = depth // (2 * B)
    q = int(round(chips**0.5))
    cz = B // nz
    taps = filter_first.shape[1]
    future = (taps // B - nz)
    groups = 2 if q > 2 else 1
    copies = (
        1 + 1 + 2 * groups + 1 + (2 * groups - 2) + 12,
        2 * groups + 1 + 2 * groups * (q - 1) + groups + 1 + (2 * groups - 2) + 4 + nz + 6,
    )
    weights = input_weight.reshape(3, chips, 2 * B, width)
    hbm = pl.BlockSpec(memory_space=pltpu.HBM)
    vmem = pl.BlockSpec(memory_space=pltpu.VMEM)
    scratch = [
        pltpu.VMEM((q, q, 2, B, B), BF16),
        pltpu.VMEM((3, chips, 2 * B, B), BF16),
        pltpu.VMEM((B, 2 * chips * B), BF16),
        pltpu.VMEM((B, 2 * chips * B), BF16),
        pltpu.VMEM((B, 3 * B), F32),
        pltpu.VMEM((2, 2, taps), BF16),
        pltpu.VMEM((B, taps), BF16),
        pltpu.VMEM((B, taps), BF16),
        pltpu.VMEM((nz, cz, B), BF16),
        pltpu.VMEM((2, nz, cz, B), BF16),
        pltpu.VMEM((nz, cz, B), BF16),
        pltpu.VMEM((2, nz, cz, B), BF16),
        pltpu.VMEM((B, taps), F32),
        pltpu.VMEM((B, taps), F32),
        pltpu.VMEM((B, B), BF16),
        pltpu.VMEM((nz, cz, B), BF16),
        pltpu.VMEM((2, nz, cz, B), BF16),
        pltpu.VMEM((future, cz, B), F32),
        pltpu.VMEM((future, cz, B), F32),
        pltpu.VMEM((nz, cz, B), F32),
        pltpu.VMEM((nz, cz, B), F32),
        pltpu.VMEM((q, q, B, B), BF16),
        pltpu.VMEM((q, H, B), F32),
        pltpu.VMEM((q, H, B), F32),
        pltpu.VMEM((q, q, H, B), BF16),
        pltpu.VMEM((q, q, H, B), BF16),
        pltpu.VMEM((q, H, B), BF16),
        pltpu.VMEM((q, H, B), BF16),
        pltpu.VMEM((q, H, B), BF16),
        pltpu.VMEM((q, H, B), BF16),
        pltpu.SemaphoreType.DMA((copies[0],)),
        pltpu.SemaphoreType.DMA((copies[1],)),
        pltpu.SemaphoreType.DMA((4,)),
        pltpu.SemaphoreType.REGULAR,
        pltpu.SemaphoreType.REGULAR,
    ]
    operands = (tokens, weights, output_weight, filter_first, filter_second)
    operands = [pltpu.with_memory_space_constraint(a, pltpu.HBM) for a in operands]
    shapes = (
            jax.ShapeDtypeStruct((B, B), BF16),
            jax.ShapeDtypeStruct((H, B), F32),
            jax.ShapeDtypeStruct((H, B), F32),
        )
    parts = pl.pallas_call(
        functools.partial(kernel, q, nz, copies),
        out_shape=shapes,
        in_specs=[hbm] * 5,
        out_specs=(vmem, vmem, vmem),
        scratch_shapes=scratch,
        compiler_params=pltpu.CompilerParams(
            collective_id=0, has_side_effects=True, vmem_limit_bytes=32 * 2**20
        ),
    )(*operands)
    return pl.pallas_call(
        finish,
        out_shape=shapes,
        in_specs=[vmem] * 3,
        out_specs=(vmem, vmem, vmem),
        compiler_params=pltpu.CompilerParams(vmem_limit_bytes=2 * 2**20),
    )(*parts)


def solution(mesh):
    in_specs = (P("seq", "ch"), P(None, None, "ch"), P("ch", None), P("ch", None), P("ch", None))
    out_specs = (P("seq", "ch"), P("seq", "ch"), P("seq", "ch"))
    return jax.shard_map(
        functools.partial(per_device, mesh.shape["seq"]),
        mesh=mesh, in_specs=in_specs, out_specs=out_specs, check_vma=False,
    )
```

```python
import functools

import jax
import jax.numpy as jnp
from jax import lax
from jax.experimental import pallas as pl
from jax.experimental.pallas import tpu as pltpu
from jax.sharding import PartitionSpec as P

MESH = pl.DeviceIdType.MESH
B = 128
H = 64
F32 = jnp.float32
BF16 = jnp.bfloat16


def build_toeplitz(taps, matrix):
    width = taps.shape[1] + B
    padded = jnp.concatenate([jnp.zeros((1, B), F32), taps], axis=1)
    rows = jnp.broadcast_to(padded, (8, width))
    row = lax.broadcasted_iota(jnp.int32, (8, width), 0)
    for bit in (1, 2, 4):
        rows = jnp.where((row & bit) != 0, pltpu.roll(rows, bit, 1), rows)
    for pair in range(B // 16):
        low = rows if pair == 0 else pltpu.roll(rows, 16 * pair, 1)
        high = pltpu.roll(rows, 16 * pair + 8, 1)
        both = jnp.concatenate([low[:, B:], high[:, B:]], axis=0)
        matrix[16 * pair : 16 * pair + 16, :] = both.astype(BF16)


def kernel(
    q, nz, copies,
    tok, wi, wo, f1, f2,
    out, ff, fs,
    X, Wv, Wown, Wsib, acc, F, M1, M2, S0, S1, G0, G1, P1, P2, U2, S2, V,
    FS1, FS2, FL1, FL2, PS, OA, OB, RA, RB, QA, QB, RA2, RB2,
    ssem, rsem, lsem, plane_ready, column_ready,
):
    cz = B // nz
    prompt = nz
    blocks = M1.shape[1] // B
    z = lax.axis_index("seq")
    ch = lax.axis_index("ch")
    core = ch % 2
    x = (ch // 2) % q
    y = ch // (2 * q)

    near = [1, q - 1] if q > 2 else [1]
    offsets = [0] + near + [e for e in range(2, q - 1)]
    slot_of = {e: i for i, e in enumerate(offsets)}
    groups = [(1, 1 + len(near))] + [(i, i + 1) for i in range(1 + len(near), q)]
    steps = offsets[1:]

    def land(e):
        return slot_of[q - e]

    def ch_of(yy, xx, cc):
        return (yy * q + xx) * 2 + cc

    def xpeer(e):
        return (z, ch_of(y, (x + e) % q, core))

    def ypeer(e):
        return (z, ch_of((y + e) % q, x, core))

    sibling = (z, ch_of(y, x, 1 - core))

    def zpeer(e):
        return ((z + e) % nz, ch)

    far_first = sorted(range(1, nz), key=lambda e: -min(e, nz - e))
    near_first = sorted(range(1, nz), key=lambda e: min(e, nz - e))

    counts = {"send": 0, "receive": 0}
    sent = []

    def fresh(kind):
        counts[kind] += 1
        return counts[kind] - 1

    def transfer(src, dst, device, s, r):
        return pltpu.make_async_remote_copy(
            src_ref=src, dst_ref=dst, send_sem=ssem.at[s], recv_sem=rsem.at[r],
            device_id=device, device_id_type=MESH,
        )

    def out_of(ref):
        s = fresh("send")
        sent.append((ref, s))
        return s

    def send(src, dst, device, s, r):
        copy = transfer(src, dst, device, s, r)
        copy.start()
        return copy

    def landed(ref, r):
        transfer(ref, ref, sibling, 0, r).wait_recv()

    own = pltpu.make_async_copy(tok, X.at[0, 0, 0], lsem.at[0])
    own.start()
    barrier = pltpu.get_barrier_semaphore()

    def greet(device):
        pl.semaphore_signal(barrier, inc=1, device_id=device, device_id_type=MESH)

    for e in steps:
        greet((z, ch_of(y, (x + e) % q, 0)))
        greet((z, ch_of((y + e) % q, x, 0)))

    @pl.when(core == 1)
    def _():
        greet(sibling)

    for e in far_first:
        greet(((z + e) % nz, ch_of(y, x, 1)))

    for i, ref in enumerate((f1, f2)):
        pltpu.make_async_copy(ref, F.at[i], lsem.at[1]).start()
    for part, k in enumerate((2, 0, 1)):
        pltpu.make_async_copy(wi.at[k], Wv.at[part], lsem.at[2]).start()
    own.wait()

    @pl.when(core == 0)
    def _():
        pl.semaphore_wait(barrier, 4 * (q - 1) + 1)
        pl.semaphore_signal(plane_ready, inc=1, device_id=sibling, device_id_type=MESH)

    @pl.when(core == 1)
    def _():
        pl.semaphore_wait(plane_ready, 1)


    s = out_of(X.at[0, 0 : q - 1])
    ag_x = [fresh("receive") for _ in groups]
    ag_y = [fresh("receive") for _ in groups]

    def group_of(slot):
        return [lo <= slot < hi for lo, hi in groups].index(True)

    for e in steps:
        g = group_of(land(e))
        send(X.at[0, 0, 0], X.at[0, land(e), 0], xpeer(e), s, ag_x[g])
        send(X.at[0, 0, 0], X.at[land(e), 0, 0], ypeer(e), s, ag_y[g])
    sib_own = send(
        X.at[0, 0, 0], X.at[0, 0, 1], sibling, out_of(X.at[0, 0, 0]), fresh("receive")
    )

    first_head = z * cz < H

    def head_taps(i):
        both = F[i].astype(F32)
        return jnp.where(first_head, both[0:1], both[1:2])

    pltpu.make_async_copy(F, F, lsem.at[1]).wait()
    build_toeplitz(head_taps(0), M1)

    sib_xy, ag_a, ag_b = [], [], []
    for g, (lo, hi) in enumerate(groups):
        s = out_of(X.at[0 : hi - lo, 0 : q - 1, 0])
        landed(X.at[0, lo:hi, 0], ag_x[g])
        ag_a.append({
            e: send(
                X.at[0, lo:hi, 0, 0:H], X.at[land(e), lo:hi, 0, 0:H], ypeer(e), s, fresh("receive")
            )
            for e in steps
        })
        landed(X.at[lo:hi, 0, 0], ag_y[g])
        ag_b.append({
            e: send(
                X.at[lo:hi, 0, 0, H:B], X.at[lo:hi, land(e), 0, H:B], xpeer(e), s, fresh("receive")
            )
            for e in steps
        })
        s, r = out_of(X.at[0, lo:hi]), fresh("receive")
        send(X.at[0, lo:hi, 0], X.at[0, lo:hi, 1], sibling, s, r)
        send(X.at[lo:hi, 0, 0], X.at[lo:hi, 0, 1], sibling, s, r)
        sib_xy.append(r)
        if g == 0:
            build_toeplitz(head_taps(1), M2)

    def chip_of(dy, dx):
        return ((y + offsets[dy]) % q) * q + (x + offsets[dx]) % q

    def terms(dy, dx, lo, hi):
        tile = jnp.concatenate([X[dy, dx, core], X[dy, dx, 1 - core]], axis=1)
        c = chip_of(dy, dx)
        weight = jnp.concatenate([Wv[part, c] for part in range(lo, hi)], axis=1)
        return jnp.dot(tile, weight, preferred_element_type=F32)

    def half_terms(dy, dx, which, lo, hi):
        c = chip_of(dy, dx)
        owner = core if which == 0 else 1 - core
        rows = pl.ds(pl.multiple_of(owner * B, B), B)
        weight = jnp.concatenate([Wv[part, c, rows, :] for part in range(lo, hi)], axis=1)
        return jnp.dot(X[dy, dx, which], weight, preferred_element_type=F32)

    def forward(g, e, s, r):
        lo, hi = groups[g]
        at = land(e)
        ag_a[g][e].wait_recv()
        send(X.at[at, lo:hi, 0, 0:H], X.at[at, lo:hi, 1, 0:H], sibling, s, r)
        ag_b[g][e].wait_recv()
        send(X.at[lo:hi, at, 0, H:B], X.at[lo:hi, at, 1, H:B], sibling, s, r)

    early = list(range(1, 1 + len(near)))
    late = list(range(1 + len(near), q))
    near_e = [e for e in range(1, q) if land(e) in early]
    far_e = [e for e in range(1, q) if land(e) in late]

    pltpu.make_async_copy(Wv, Wv, lsem.at[2]).wait()
    sib_own.wait_recv()
    total = terms(0, 0, 0, 3)
    landed(X.at[0, 1 : 1 + len(near)], sib_xy[0])
    for d in early:
        total += terms(0, d, 0, 3)
        total += terms(d, 0, 0, 3)
    acc[...] = total
    corner = X.at[1 : 1 + len(near), 1 : 1 + len(near), 1]
    s, first_fwd = out_of(corner), fresh("receive")
    for e in near_e:
        forward(0, e, s, first_fwd)
    last_fwd = []
    if far_e:
        ref = X.at[1 + len(near) : q, 1 : 1 + len(near), 1]
        s, r = out_of(ref), fresh("receive")
        last_fwd.append((ref, r))
        for e in far_e:
            forward(0, e, s, r)
    for g in range(1, len(groups)):
        lo, hi = groups[g]
        ref = X.at[lo:hi, 1:q, 1]
        s, r = out_of(ref), fresh("receive")
        last_fwd.append((ref, r))
        for e in near_e + far_e:
            forward(g, e, s, r)

    @pl.when(core == 1)
    def _():
        pl.semaphore_wait(barrier, 2 * (nz - 1))
        pl.semaphore_signal(column_ready, inc=1, device_id=sibling, device_id_type=MESH)

    total = acc[...]
    for g in range(1, len(groups)):
        landed(X.at[0, groups[g][0] : groups[g][1]], sib_xy[g])
        for d in range(*groups[g]):
            total += terms(0, d, 0, 3)
            total += terms(d, 0, 0, 3)
    landed(corner, first_fwd)
    for dy in early:
        for dx in early:
            total += terms(dy, dx, 0, 3)
    rest = [(dy, dx) for dy in range(1, q) for dx in range(1, q) if dy in late or dx in late]
    for dy, dx in rest:
        total += half_terms(dy, dx, 0, 0, 3)
    acc[...] = total
    for ref, r in last_fwd:
        landed(ref, r)

    @pl.when(core == 0)
    def _():
        pl.semaphore_wait(column_ready, 1)


    total = acc[:, 0:B]
    for dy, dx in rest:
        total += half_terms(dy, dx, 1, 0, 1)
    S0[...] = jnp.transpose(total).astype(BF16).reshape(nz, cz, B)
    s, value_in = out_of(S0.at[0 : nz - 1]), fresh("receive")
    for e in far_first:
        send(S0.at[(z + e) % nz], G0.at[z], zpeer(e), s, value_in)
    G0[z] = S0[z]
    gates_in = []
    for part in range(2):
        total = acc[:, part * B + B : part * B + 2 * B]
        for dy, dx in rest:
            total += half_terms(dy, dx, 1, part + 1, part + 2)
        S1[part] = jnp.transpose(total).astype(BF16).reshape(nz, cz, B)
        s, r = out_of(S1.at[part, 0 : nz - 1]), fresh("receive")
        for e in far_first:
            send(S1.at[part, (z + e) % nz], G1.at[part, z], zpeer(e), s, r)
        G1[part, z] = S1[part, z]
        gates_in.append(r)

    own_rows = pltpu.make_async_copy(wo, Wown, lsem.at[3])
    own_rows.start()
    sibling_rows = send(wo, Wsib, sibling, out_of(Wsib), fresh("receive"))

    def conv_block(P_ref, t):
        total = None
        for s in range(nz):
            if 0 <= t - s < blocks:
                term = P_ref[s * cz : s * cz + cz, (t - s) * B : (t - s) * B + B]
                total = term if total is None else total + term
        return total

    landed(G0.at[0 : nz - 1], value_in)
    signal = G0[...].reshape(B, B)
    P1[:, : prompt * B] = jnp.dot(signal, M1[:, : prompt * B], preferred_element_type=F32)
    landed(G1.at[0, 0 : nz - 1], gates_in[0])
    for t in range(prompt):
        mixed = (G1[0, t].astype(F32) * conv_block(P1, t)).astype(BF16)
        U2[t * cz : t * cz + cz, :] = mixed
    P2[:, : prompt * B] = jnp.dot(U2[...], M2[:, : prompt * B], preferred_element_type=F32)
    landed(G1.at[1, 0 : nz - 1], gates_in[1])
    for t in range(prompt):
        S2[t] = (G1[1, t].astype(F32) * conv_block(P2, t)).astype(BF16)
    s = out_of(S2.at[0 : nz - 1])
    back = {
        e: send(S2.at[(z + e) % nz], V.at[0, z], zpeer(e), s, fresh("receive")) for e in far_first
    }
    s, fwd = out_of(V.at[1]), fresh("receive")
    send(S2.at[z], V.at[1, z], sibling, s, fwd)
    V[0, z] = S2[z]
    for sig, M_ref, P_ref, FS in ((signal, M1, P1, FS1), (U2[...], M2, P2, FS2)):
        P_ref[:, prompt * B :] = jnp.dot(sig, M_ref[:, prompt * B :], preferred_element_type=F32)
        for t in range(prompt, blocks):
            FS[t - prompt] = conv_block(P_ref, t)
    own_rows.wait()
    sibling_rows.wait_recv()
    for e in near_first:
        back[e].wait_recv()
        source = (z + nz - e) % nz
        send(V.at[0, source], V.at[1, source], sibling, s, fwd)
    own_half = jnp.transpose(V[0].reshape(B, B).astype(F32)).astype(BF16)
    landed(V.at[1], fwd)

    other_half = jnp.transpose(V[1].reshape(B, B).astype(F32)).astype(BF16)
    mixed = jnp.concatenate([own_half, other_half], axis=1)

    def out_block(dy, dx):
        c = chip_of(dy, dx)
        columns = pl.ds(pl.multiple_of((2 * c + core) * B, B), B)
        weight = jnp.concatenate([Wown[:, columns], Wsib[:, columns]], axis=0)
        block = jnp.dot(mixed, weight, preferred_element_type=F32)
        if dx == 0:
            OA[dy] = block[0:H]
        if dy == 0:
            OB[dx] = block[H:B]
        if dx or dy:
            PS[dy, dx] = block.astype(BF16)

    done = set()
    (sa, rs_a), (sb, rs_b) = ((out_of(R.at[1:q]), fresh("receive")) for R in (RA, RB))
    for e in reversed(steps):
        s = slot_of[e]
        for d in range(q):
            for at in ((d, s), (s, d)):
                if at not in done:
                    done.add(at)
                    out_block(*at)
            if d == q - 1:
                send(PS.at[:, s, 0:H], RA.at[land(e)], xpeer(e), sa, rs_a)
                send(PS.at[s, :, H:B], RB.at[land(e)], ypeer(e), sb, rs_b)
    out_block(0, 0)

    future = []
    for FS, FL in ((FS1, FL1), (FS2, FL2)):
        s, r = out_of(FL.at[0 : nz - 1]), fresh("receive")
        for e in far_first:
            send(FS.at[((z + e) % nz) // 2], FL.at[z], zpeer(e), s, r)
        future.append(r)
        FL[z] = FS[z // 2]

    def gather_sums(r, O, R, Q):
        landed(R.at[1:q], r)
        for d in range(q):
            total = O[d]
            for e in range(1, q):
                total += R[e, d].astype(F32)
            if d == 0:
                O[d] = total
            else:
                Q[d] = total.astype(BF16)

    gather_sums(rs_a, OA, RA, QA)
    s, rs_a2 = out_of(RA2.at[1:q]), fresh("receive")
    for e in reversed(steps):
        send(QA.at[slot_of[e]], RA2.at[land(e)], ypeer(e), s, rs_a2)
    gather_sums(rs_b, OB, RB, QB)
    s, rs_b2 = out_of(RB2.at[1:q]), fresh("receive")
    for e in reversed(steps):
        send(QB.at[slot_of[e]], RB2.at[land(e)], xpeer(e), s, rs_b2)

    for r, FL, ref in zip(future, (FL1, FL2), (ff, fs)):
        landed(FL.at[0 : nz - 1], r)
        rows = jnp.transpose(FL[...].reshape(B, B))
        ref[...] = jnp.where(z % 2 == 0, rows[0:H], rows[H:B])

    for r, O, R, rows in ((rs_a2, OA, RA2, slice(0, H)), (rs_b2, OB, RB2, slice(H, B))):
        landed(R.at[1:q], r)
        total = O[0]
        for e in range(1, q):
            total += R[e].astype(F32)
        out[rows, :] = total.astype(BF16)

    for ref, s in sent:
        transfer(ref, ref, sibling, s, 0).wait_send()
    assert counts == {"send": copies[0], "receive": copies[1]}, counts


def finish(a, b, c, out, ff, fs):
    out[...] = a[...]
    ff[...] = b[...]
    fs[...] = c[...]


def per_device(nz, tokens, input_weight, output_weight, filter_first, filter_second):
    depth, width = input_weight.shape[1:]
    chips = depth // (2 * B)
    q = int(round(chips**0.5))
    cz = B // nz
    taps = filter_first.shape[1]
    future = (taps // B - nz)
    groups = 2 if q > 2 else 1
    copies = (
        1 + 1 + 2 * groups + 1 + (2 * groups - 2) + 12,
        2 * groups + 1 + 2 * groups * (q - 1) + groups + 1 + (2 * groups - 2) + 4 + nz + 6,
    )
    weights = input_weight.reshape(3, chips, 2 * B, width)
    hbm = pl.BlockSpec(memory_space=pltpu.HBM)
    vmem = pl.BlockSpec(memory_space=pltpu.VMEM)
    scratch = [
        pltpu.VMEM((q, q, 2, B, B), BF16),
        pltpu.VMEM((3, chips, 2 * B, B), BF16),
        pltpu.VMEM((B, 2 * chips * B), BF16),
        pltpu.VMEM((B, 2 * chips * B), BF16),
        pltpu.VMEM((B, 3 * B), F32),
        pltpu.VMEM((2, 2, taps), BF16),
        pltpu.VMEM((B, taps), BF16),
        pltpu.VMEM((B, taps), BF16),
        pltpu.VMEM((nz, cz, B), BF16),
        pltpu.VMEM((2, nz, cz, B), BF16),
        pltpu.VMEM((nz, cz, B), BF16),
        pltpu.VMEM((2, nz, cz, B), BF16),
        pltpu.VMEM((B, taps), F32),
        pltpu.VMEM((B, taps), F32),
        pltpu.VMEM((B, B), BF16),
        pltpu.VMEM((nz, cz, B), BF16),
        pltpu.VMEM((2, nz, cz, B), BF16),
        pltpu.VMEM((future, cz, B), F32),
        pltpu.VMEM((future, cz, B), F32),
        pltpu.VMEM((nz, cz, B), F32),
        pltpu.VMEM((nz, cz, B), F32),
        pltpu.VMEM((q, q, B, B), BF16),
        pltpu.VMEM((q, H, B), F32),
        pltpu.VMEM((q, H, B), F32),
        pltpu.VMEM((q, q, H, B), BF16),
        pltpu.VMEM((q, q, H, B), BF16),
        pltpu.VMEM((q, H, B), BF16),
        pltpu.VMEM((q, H, B), BF16),
        pltpu.VMEM((q, H, B), BF16),
        pltpu.VMEM((q, H, B), BF16),
        pltpu.SemaphoreType.DMA((copies[0],)),
        pltpu.SemaphoreType.DMA((copies[1],)),
        pltpu.SemaphoreType.DMA((4,)),
        pltpu.SemaphoreType.REGULAR,
        pltpu.SemaphoreType.REGULAR,
    ]
    operands = (tokens, weights, output_weight, filter_first, filter_second)
    operands = [pltpu.with_memory_space_constraint(a, pltpu.HBM) for a in operands]
    shapes = (
            jax.ShapeDtypeStruct((B, B), BF16),
            jax.ShapeDtypeStruct((H, B), F32),
            jax.ShapeDtypeStruct((H, B), F32),
        )
    parts = pl.pallas_call(
        functools.partial(kernel, q, nz, copies),
        out_shape=shapes,
        in_specs=[hbm] * 5,
        out_specs=(vmem, vmem, vmem),
        scratch_shapes=scratch,
        compiler_params=pltpu.CompilerParams(
            collective_id=0, has_side_effects=True, vmem_limit_bytes=32 * 2**20
        ),
    )(*operands)
    return pl.pallas_call(
        finish,
        out_shape=shapes,
        in_specs=[vmem] * 3,
        out_specs=(vmem, vmem, vmem),
        compiler_params=pltpu.CompilerParams(vmem_limit_bytes=2 * 2**20),
    )(*parts)


def solution(mesh):
    in_specs = (P("seq", "ch"), P(None, None, "ch"), P("ch", None), P("ch", None), P("ch", None))
    out_specs = (P("seq", "ch"), P("seq", "ch"), P("seq", "ch"))
    return jax.shard_map(
        functools.partial(per_device, mesh.shape["seq"]),
        mesh=mesh, in_specs=in_specs, out_specs=out_specs, check_vma=False,
    )
```
